32 devices in a mesh: dp: 2 (over core), ret: 4 (over y, x), ctx: 4 (over z).
Axes of the slice: x: 2, y: 2, z: 4, core: 2. Of those that a mesh axis runs over, the one named last changes fastest.
Arguments:
- queries: bfloat16 [2, 2048, 4096], P('dp', 'ret', 'ctx'), may hold values from -6 to 6
- enc_states: bfloat16 [2, 8192, 896], P('dp', 'ret'), may hold values from -1600 to 1600
- w_key: bfloat16 [896, 4096], P(None, 'ctx'), may hold values from -0.1875 to 0.1875
- w_value: bfloat16 [896, 4096], P(None, 'ctx'), may hold values from -0.59765625 to 0.59765625
- shard_ids: int32 [2, 32, 2], P('dp', 'ret'), may hold values from 0 to 3, all different within a row; in each aligned block of 8 rows (0 to 7, 8 to 15, ..., all dimensions but the last counted through in order) at most 8 rows name the same one
- row_ids: int32 [2, 32, 2], P('dp', 'ret'), may hold values from 0 to 15
- grad_out: bfloat16 [2, 2048, 4096], P('dp', 'ret', 'ctx'), may hold values from -6 to 6
Outputs:
- attended: bfloat16 [2, 2048, 4096], P('dp', 'ret', 'ctx')
- grad_queries: bfloat16 [2, 2048, 4096], P('dp', 'ret', 'ctx')
- grad_w_key: float32 [896, 4096], P(('dp', 'ret'), 'ctx')
- grad_w_value: float32 [896, 4096], P(('dp', 'ret'), 'ctx')
The draws below stay inside these ranges and needn't reach their ends.
Inputs may be any that keep to these rules, and one draw needn't show every extreme that they name: `shard_ids`: each block names 2 different shards; among the 8 blocks that one index of ret holds, no shard is named by more than 8 blocks, a bound that some block reaches.
All inputs are finite; a program needn't handle non-finite values.
Results may differ from the reference program's by a relative error of at most 0.019.
Values may be sent and summed in bfloat16 or wider, within the bound.
No kernel may reach another device: no remote copies, remote signals or barrier semaphores. Data moves between devices by JAX's collectives and lax.ppermute only.
A program may use at most 128 MiB of HBM per device.

```python
import math
import jax
import jax.numpy as jnp
import numpy as np
from jax import lax

HEADS = 32
HEAD_DIM = 128
ENC_WIDTH = 896
BLOCK_LEN = 64
NEIGH_LEN = 128
NEIGHBOURS = 2
BLOCKS_DEV = 8
DB_DEV = 16
CAPACITY = 8
BATCH = 2
BLOCKS = 32
SEQ_LEN = 2048
N_RET = 4


def draw_queries(key, part):
    second = jax.random.fold_in(key, 1)
    shape = (BATCH, SEQ_LEN, HEADS * HEAD_DIM)
    base = jnp.clip(jax.random.normal(second, shape, jnp.float32), -4.0, 4.0) * 1.5
    return base.astype(jnp.bfloat16)


def draw_enc_states(key, part):
    keys_list = jax.random.split(key, 6)
    db_rows = N_RET * DB_DEV * NEIGH_LEN
    shape = (BATCH, db_rows, ENC_WIDTH)
    row_scale = jnp.exp(jax.random.uniform(keys_list[0], (BATCH, db_rows, 1), jnp.float32, 0.0, math.log(10.0)))
    col_scale = jnp.exp(jax.random.uniform(keys_list[1], (BATCH, 1, ENC_WIDTH), jnp.float32, 0.0, math.log(10.0)))
    block_total = BATCH * N_RET
    pairing = jax.random.permutation(keys_list[2], block_total)
    batch_index = jnp.arange(BATCH, dtype=jnp.int32)[:, None, None]
    row_index = jnp.arange(db_rows, dtype=jnp.int32)[None, :, None]
    row_block = batch_index * N_RET + row_index // (DB_DEV * NEIGH_LEN)
    col_block = (jnp.arange(ENC_WIDTH, dtype=jnp.int32) // (ENC_WIDTH // block_total))[None, None, :]
    spike = jnp.where(pairing[row_block] == col_block, 4.0, 1.0)
    base = jnp.clip(jax.random.normal(keys_list[5], shape, jnp.float32), -4.0, 4.0)
    return (base * row_scale * col_scale * spike).astype(jnp.bfloat16)


def with_ends(array, rng, smallest, top_value):
    dims = array.shape
    index_at = [jax.random.randint(jax.random.fold_in(rng, axis), (), 0, dims[axis]) for axis in range(len(dims))]
    array = array.at[tuple(index_at)].set(smallest)
    longest = dims.index(max(dims))
    index_at[longest] = (index_at[longest] + 1) % dims[longest]
    return array.at[tuple(index_at)].set(top_value)


def shard_levels(own_key, extent, cuts, low, top_value):
    factor_of = 1.0
    for position, blocks in cuts:
        heights = jax.random.uniform(jax.random.fold_in(jax.random.fold_in(own_key, 6), position), (blocks,), jnp.float32, low / len(cuts), top_value / len(cuts))
        factor_of = factor_of * jnp.repeat(jnp.exp(heights), extent[position] // blocks).reshape((-1,) + (1,) * (len(extent) - 1 - position))
    return factor_of


def deal_out(stream_key, own, number, rows, count, top, limit, skew):
    order = jax.random.permutation(stream_key, count)
    crowded, ordinary = shares(count, rows * top, limit, skew, True), shares(count, rows * top, limit, skew, False)
    places = jnp.arange(count)

    def named(lengths, turn):
        used = int((lengths > 0).sum())
        fixed = max(1, used // 4)
        shifted = fixed + (places - fixed + turn * (used - fixed)) % max(1, count - fixed)
        return jnp.zeros((count,), jnp.int32).at[order[jnp.where(places < fixed, places, shifted)]].set(jnp.asarray(lengths, jnp.int32))

    lengths = jnp.where(number % 4 == 0, named(crowded, number // 4), named(ordinary, number - number // 4 - 1))
    mixed = jax.random.permutation(jax.random.fold_in(own, 3), count)
    giver, sink = mixed[0:count // 2 * 2:2], mixed[1:count // 2 * 2:2]
    slack = jnp.minimum(lengths[giver] - 1, limit - lengths[sink]) // 2
    slack = jnp.where((giver == order[0]) | (sink == order[0]) | (lengths[sink] == 0), 0, jnp.maximum(slack, 0))
    shifted = jax.random.randint(jax.random.fold_in(own, 4), (count // 2,), 0, 1 << 20) % (slack + 1)
    lengths = lengths.at[giver].add(-shifted).at[sink].add(shifted)
    members = jnp.searchsorted(jnp.cumsum(lengths), jnp.arange(rows * top), side="right").astype(jnp.int32)
    listing = members.reshape(top, rows).T
    listing = listing[jax.random.permutation(jax.random.fold_in(own, 1), rows)]
    turn = jax.random.randint(jax.random.fold_in(own, 2), (rows, 1), 0, top)
    return jnp.take_along_axis(listing, (jnp.arange(top)[None, :] + turn) % top, axis=1)


def shares(count, total, reach, slope, full):
    portions = [(1 << 20) // math.isqrt(rank ** slope) + 1 for rank in range(1, count + 1)]
    largest = reach if full else min(reach, max(-(-total // count), total * portions[0] // sum(portions)))
    least = 1 if total - largest >= count - 1 else 0
    holding, rest = [largest] + [least] * (count - 1), total - largest - least * (count - 1)
    while rest > 0:
        candidates = [i for i in range(1, count) if holding[i] < largest] or [i for i in range(1, count) if holding[i] < reach]
        pool, budget = sum([portions[i] for i in candidates]), rest
        for i in candidates:
            more = min(reach - holding[i], max(1, budget * portions[i] // pool), rest)
            holding[i] = holding[i] + more
            rest = rest - more
    return np.array(holding)


def noise(key, dims, scale, reach, pieces=(), kind=jnp.bfloat16):
    gain = shard_levels(key, dims, pieces, -0.22, 0.18) if pieces else 1.0
    drawn = jax.random.normal(key, dims, jnp.float32) * scale * gain
    return jnp.minimum(jnp.maximum(drawn, -reach), reach).astype(kind)


def setup_inputs(seed: int = 0) -> dict:
    seeds = jax.random.split(jax.random.key(seed), 8)
    queries = draw_queries(jax.random.fold_in(seeds[7], 71), 0)
    enc_states = draw_enc_states(jax.random.fold_in(seeds[7], 71), 0)
    w_key = noise(seeds[2], (ENC_WIDTH, HEADS * HEAD_DIM), ENC_WIDTH ** -0.5, 0.1875, ((1, 4),))
    w_value = noise(seeds[3], (ENC_WIDTH, HEADS * HEAD_DIM), (3.0 / ENC_WIDTH ** 0.5), 0.59765625, ((1, 4),))
    shard_ids_keys = jax.random.split(jax.random.fold_in(seeds[4], 1), BATCH * BLOCKS // BLOCKS_DEV)
    shard_ids_turns = jax.random.permutation(jax.random.fold_in(seeds[4], 3), BATCH * BLOCKS // BLOCKS_DEV)
    shard_ids = jax.vmap(lambda own, number: deal_out(jax.random.fold_in(seeds[4], 2), own, number, BLOCKS_DEV, N_RET, NEIGHBOURS, CAPACITY, 2))(shard_ids_keys, shard_ids_turns).reshape((BATCH, BLOCKS, NEIGHBOURS))
    row_ids = with_ends(jax.random.randint(seeds[5], (BATCH, BLOCKS, NEIGHBOURS), 0, DB_DEV), jax.random.fold_in(seeds[5], 1), 0, DB_DEV - 1).astype(jnp.int32)
    grad_out = noise(seeds[6], (BATCH, SEQ_LEN, HEADS * HEAD_DIM), 1.0, 6.0, ((0, 2), (1, 4), (2, 4)))
    return dict(queries=queries, enc_states=enc_states, w_key=w_key, w_value=w_value, shard_ids=shard_ids, row_ids=row_ids, grad_out=grad_out)


def rounded(tensor):
    return lax.optimization_barrier(tensor.astype(jnp.bfloat16)).astype(jnp.float32)

def normalize_rows(states):
    floats = states.astype(jnp.float32)
    mean_square = lax.optimization_barrier(jnp.mean(floats * floats, axis=-1, keepdims=True))
    return (floats * lax.rsqrt(mean_square + 1e-06)).astype(jnp.bfloat16)

def contract_rows(lhs_rows, rhs_rows):
    return lax.dot_general(lhs_rows, rhs_rows, (((0,), (0,)), ((), ())), preferred_element_type=jnp.float32)

def block_attention(query_block, key_block, value_block, grad_block):
    score_scale = 1.0 / math.sqrt(HEAD_DIM)
    query_f = query_block.astype(jnp.float32)
    key_f = key_block.astype(jnp.float32)
    value_f = value_block.astype(jnp.float32)
    grad_f = grad_block.astype(jnp.float32)
    scores = jnp.einsum('thd,jhd->htj', query_f, key_f) * score_scale
    exponent = jnp.exp(scores)
    denominator = lax.optimization_barrier(jnp.sum(exponent, axis=-1))
    numerator = jnp.einsum('htj,jhd->thd', rounded(exponent), value_f)
    output = numerator / jnp.transpose(denominator)[:, :, None]
    prob_grad = jnp.einsum('thd,jhd->htj', grad_f, value_f)
    row_delta = jnp.transpose(lax.optimization_barrier(jnp.sum(grad_f * output, axis=-1)))
    probability = exponent / denominator[:, :, None]
    score_grad = rounded(probability * (prob_grad - row_delta[:, :, None]) * score_scale)
    grad_query = jnp.einsum('htj,jhd->thd', score_grad, key_f).astype(jnp.bfloat16)
    grad_key = jnp.einsum('htj,thd->jhd', score_grad, query_f).astype(jnp.bfloat16)
    grad_value = jnp.einsum('htj,thd->jhd', rounded(probability), grad_f).astype(jnp.bfloat16)
    return (output.astype(jnp.bfloat16), grad_query, grad_key, grad_value)

def reference(queries, enc_states, w_key, w_value, shard_ids, row_ids, grad_out):
    feat_width = HEADS * HEAD_DIM
    context_rows = NEIGHBOURS * NEIGH_LEN
    attended_list = []
    grad_list = []
    sum_key = jnp.zeros((ENC_WIDTH, feat_width), jnp.float32)
    sum_value = jnp.zeros((ENC_WIDTH, feat_width), jnp.float32)
    for replica in range(queries.shape[0]):
        normed = lax.optimization_barrier(normalize_rows(enc_states[replica]))
        key_table = lax.optimization_barrier(jnp.dot(normed, w_key, preferred_element_type=jnp.float32).astype(jnp.bfloat16)).reshape(N_RET * DB_DEV, NEIGH_LEN, HEADS, HEAD_DIM)
        value_table = lax.optimization_barrier(jnp.dot(normed, w_value, preferred_element_type=jnp.float32).astype(jnp.bfloat16)).reshape(N_RET * DB_DEV, NEIGH_LEN, HEADS, HEAD_DIM)
        normed_table = normed.reshape(N_RET * DB_DEV, NEIGH_LEN, ENC_WIDTH)
        neighbour = (shard_ids[replica] * DB_DEV + row_ids[replica]).astype(jnp.int32)
        query_blocks = queries[replica].reshape(BLOCKS, BLOCK_LEN, HEADS, HEAD_DIM)
        grad_blocks = grad_out[replica].reshape(BLOCKS, BLOCK_LEN, HEADS, HEAD_DIM)

        def block_step(running, inputs):
            query_block, grad_block, chosen = inputs
            key_block = key_table[chosen].reshape(context_rows, HEADS, HEAD_DIM)
            value_block = value_table[chosen].reshape(context_rows, HEADS, HEAD_DIM)
            output, grad_query, grad_key, grad_value = block_attention(query_block, key_block, value_block, grad_block)
            state_rows = normed_table[chosen].reshape(context_rows, ENC_WIDTH)
            key_sum = running[0] + contract_rows(state_rows, grad_key.reshape(context_rows, feat_width))
            value_sum = running[1] + contract_rows(state_rows, grad_value.reshape(context_rows, feat_width))
            return ((key_sum, value_sum), (output, grad_query))
        (sum_key, sum_value), (outputs, grads) = lax.scan(block_step, (sum_key, sum_value), (query_blocks, grad_blocks, neighbour))
        attended_list.append(outputs.reshape(SEQ_LEN, feat_width))
        grad_list.append(grads.reshape(SEQ_LEN, feat_width))
    return (jnp.stack(attended_list), jnp.stack(grad_list), sum_key, sum_value)
```

```python
import functools
import math

import jax
import jax.numpy as jnp
from jax import lax
from jax.experimental import pallas as pl
from jax.experimental.pallas import tpu as pltpu
from jax.sharding import PartitionSpec as P

HEAD_DIM = 128
NEIGH_LEN = 128
NEIGHBOURS = 2
VMEM_BYTES = 56 * 1024 * 1024

F32 = jnp.float32
BF16 = jnp.bfloat16


def contract(lhs, rhs, dims):
    return lax.dot_general(lhs, rhs, (dims, ((), ())), preferred_element_type=F32)


def normalize_rows(states):
    floats = states.astype(F32)
    mean_square = jnp.mean(floats * floats, axis=-1, keepdims=True)
    return (floats * lax.rsqrt(mean_square + 1e-06)).astype(BF16)


def block_grads(context, wk_ref, wv_ref, q_ref, go_ref, out_ref, gq_ref, dk_ref, dv_ref):
    score_scale = 1.0 / math.sqrt(HEAD_DIM)
    keys = jnp.dot(context, wk_ref[...], preferred_element_type=F32).astype(BF16)
    values = jnp.dot(context, wv_ref[...], preferred_element_type=F32).astype(BF16)
    for head in range(q_ref.shape[1] // HEAD_DIM):
        cols = slice(head * HEAD_DIM, (head + 1) * HEAD_DIM)
        key, value, query, grad = keys[:, cols], values[:, cols], q_ref[:, cols], go_ref[:, cols]
        expo = jnp.exp(contract(query, key, ((1,), (1,))) * score_scale)
        inverse = 1.0 / jnp.sum(expo, axis=-1, keepdims=True)
        output = jnp.dot(expo.astype(BF16), value, preferred_element_type=F32) * inverse
        out_ref[:, cols] = output.astype(BF16)
        dprob = contract(grad, value, ((1,), (1,)))
        delta = jnp.sum(grad.astype(F32) * output, axis=-1, keepdims=True)
        probs = expo * inverse
        dscore = (probs * (dprob - delta) * score_scale).astype(BF16)
        gq_ref[:, cols] = jnp.dot(dscore, key, preferred_element_type=F32).astype(BF16)
        dk_ref[:, cols] = contract(dscore, query, ((0,), (0,))).astype(BF16)
        dv_ref[:, cols] = contract(probs.astype(BF16), grad, ((0,), (0,))).astype(BF16)


def attend_kernel(
    slot_ref, first_ref, second_ref, wk_ref, wv_ref, q_ref, go_ref,
    out_ref, gq_ref, dwk_ref, dwv_ref, acck, accv, dk_ref, dv_ref,
):
    step = pl.program_id(0)

    @pl.when(step == 0)
    def _():
        acck[...] = jnp.zeros_like(acck)
        accv[...] = jnp.zeros_like(accv)

    width = first_ref.shape[-1]
    context = jnp.concatenate([first_ref[...].reshape(-1, width), second_ref[...].reshape(-1, width)], axis=0)
    block_grads(context, wk_ref, wv_ref, q_ref, go_ref, out_ref, gq_ref, dk_ref, dv_ref)
    acck[...] += contract(context, dk_ref[...], ((0,), (0,)))
    accv[...] += contract(context, dv_ref[...], ((0,), (0,)))

    @pl.when(step == pl.num_programs(0) - 1)
    def _():
        dwk_ref[...] = acck[...].astype(dwk_ref.dtype)
        dwv_ref[...] = accv[...].astype(dwv_ref.dtype)


def attend(incoming, slots, wk, wv, queries, grad_out):
    count = slots.shape[0]
    tokens, feat = queries.shape[0] // count, queries.shape[1]
    enc = wk.shape[0]
    whole = lambda shape: pl.BlockSpec(shape, lambda b, s: (0, 0))
    row_spec = pl.BlockSpec((tokens, feat), lambda b, s: (b, 0))
    neigh = lambda n: pl.BlockSpec((1, NEIGH_LEN, enc), lambda b, s: (s[b, n], 0, 0))
    return pl.pallas_call(
        attend_kernel,
        grid_spec=pltpu.PrefetchScalarGridSpec(
            num_scalar_prefetch=1,
            grid=(count,),
            in_specs=[neigh(0), neigh(1), whole((enc, feat)), whole((enc, feat)), row_spec, row_spec],
            out_specs=[row_spec, row_spec, whole((enc, feat)), whole((enc, feat))],
            scratch_shapes=[
                pltpu.VMEM((enc, feat), F32),
                pltpu.VMEM((enc, feat), F32),
                pltpu.VMEM((NEIGHBOURS * NEIGH_LEN, feat), BF16),
                pltpu.VMEM((NEIGHBOURS * NEIGH_LEN, feat), BF16),
            ],
        ),
        out_shape=[
            jax.ShapeDtypeStruct(queries.shape, BF16),
            jax.ShapeDtypeStruct(queries.shape, BF16),
            jax.ShapeDtypeStruct((enc, feat), BF16),
            jax.ShapeDtypeStruct((enc, feat), BF16),
        ],
        compiler_params=pltpu.CompilerParams(vmem_limit_bytes=VMEM_BYTES),
        name="attend_blocks",
    )(slots, incoming, incoming, wk, wv, queries, grad_out)


def pick_kernel(id_ref, normed_ref, out_ref):
    me = lax.axis_index("ret")
    for dest in range(out_ref.shape[0]):
        def body(req, used, dest=dest):
            mine = id_ref[dest, req, 0] == me

            @pl.when(mine)
            def _():
                out_ref[dest, used] = normed_ref[id_ref[dest, req, 1]]

            return used + jnp.where(mine, 1, 0)

        lax.fori_loop(0, id_ref.shape[1], body, jnp.int32(0))


def pick(ids, normed, capacity):
    n_ret = ids.shape[0]
    return pl.pallas_call(
        pick_kernel,
        in_specs=[pl.BlockSpec(memory_space=pltpu.SMEM), pl.BlockSpec(memory_space=pltpu.VMEM)],
        out_specs=pl.BlockSpec(memory_space=pltpu.VMEM),
        out_shape=jax.ShapeDtypeStruct((n_ret, capacity) + normed.shape[1:], BF16),
        compiler_params=pltpu.CompilerParams(vmem_limit_bytes=VMEM_BYTES),
        name="pick_rows",
    )(ids, normed)


def own_slots(shards, capacity):
    flat = shards.reshape(-1)
    place = jnp.arange(flat.shape[0], dtype=jnp.int32)
    earlier = (flat[:, None] == flat[None, :]) & (place[None, :] < place[:, None])
    return (flat * capacity + jnp.sum(earlier.astype(jnp.int32), axis=1)).reshape(shards.shape)


def local(queries, enc_states, w_key, w_value, shard_ids, row_ids, grad_out):
    n_ret = lax.axis_size("ret")
    blocks = shard_ids.shape[1]
    capacity = min(blocks, 2 * blocks * NEIGHBOURS // n_ret)
    enc = enc_states.shape[2]
    feat = queries.shape[2]
    own = jnp.stack([shard_ids[0], row_ids[0]], axis=-1).reshape(-1, 2)
    ids = lax.all_gather(own, "ret")
    normed = normalize_rows(enc_states[0]).reshape(-1, NEIGH_LEN, enc)
    outgoing = pick(ids, normed, capacity)
    incoming = lax.all_to_all(outgoing, "ret", split_axis=0, concat_axis=0, tiled=True)
    slots = own_slots(shard_ids[0], capacity)
    attended, grad_queries, dwk, dwv = attend(
        incoming.reshape(-1, NEIGH_LEN, enc), slots, w_key, w_value, queries[0], grad_out[0]
    )
    both = jnp.concatenate([dwk, dwv], axis=1)
    summed = lax.psum_scatter(both, ("dp", "ret"), scatter_dimension=0, tiled=True).astype(F32)
    return attended[None], grad_queries[None], summed[:, :feat], summed[:, feat:]


def solution(mesh):
    placed = (
        P("dp", "ret", "ctx"),
        P("dp", "ret", None),
        P(None, "ctx"),
        P(None, "ctx"),
        P("dp", "ret", None),
        P("dp", "ret", None),
        P("dp", "ret", "ctx"),
    )
    return jax.shard_map(
        local,
        mesh=mesh,
        in_specs=placed,
        out_specs=(
            P("dp", "ret", "ctx"),
            P("dp", "ret", "ctx"),
            P(("dp", "ret"), "ctx"),
            P(("dp", "ret"), "ctx"),
        ),
        check_vma=False,
    )
```

```python
import functools
import math

import jax
import jax.numpy as jnp
from jax import lax
from jax.experimental import pallas as pl
from jax.experimental.pallas import tpu as pltpu
from jax.sharding import PartitionSpec as P

HEAD_DIM = 128
NEIGH_LEN = 128
NEIGHBOURS = 2
HALF = NEIGH_LEN // 2
MIB = 1024 * 1024
ATTEND_MIB = 32
CHUNKS = ((3, True), (3, True), (2, False))

F32 = jnp.float32
BF16 = jnp.bfloat16
ANY = pl.BlockSpec(memory_space=pl.ANY)
SMEM = pl.BlockSpec(memory_space=pltpu.SMEM)
VMEM = pl.BlockSpec(memory_space=pltpu.VMEM)
HBM = pl.BlockSpec(memory_space=pltpu.HBM)


def params(mib):
    return pltpu.CompilerParams(vmem_limit_bytes=mib * MIB)


def contract(lhs, rhs, dims):
    return lax.dot_general(lhs, rhs, (dims, ((), ())), preferred_element_type=F32)


def swap(array, axis, bit):
    size = lax.axis_size(axis)
    return lax.ppermute(array, axis, [(i, i ^ bit) for i in range(size)])


def normalize_kernel(states_ref, out_ref):
    floats = states_ref[...].astype(F32)
    mean_square = jnp.mean(floats * floats, axis=-1, keepdims=True)
    out_ref[...] = (floats * lax.rsqrt(mean_square + 1e-06)).astype(BF16)


def normalize_rows(states):
    rows, width = states.shape
    tile = 512
    spec = pl.BlockSpec((tile, width), lambda i: (i, 0))
    return pl.pallas_call(
        normalize_kernel,
        grid=(rows // tile,),
        in_specs=[spec],
        out_specs=spec,
        out_shape=jax.ShapeDtypeStruct(states.shape, BF16),
        compiler_params=params(12),
        name="normalize_rows",
    )(states)


def exchange_ids(own):
    n_ret = lax.axis_size("ret")
    if n_ret <= 4:
        return jnp.stack([own] + [swap(own, "ret", k) for k in range(1, n_ret)])
    every = lax.all_gather(own, "ret")
    order = jnp.arange(n_ret, dtype=jnp.int32) ^ lax.axis_index("ret")
    return jnp.take(every, order, axis=0)


def pick_kernel(spans, id_ref, normed_ref, *refs):
    n_ret = id_ref.shape[0]
    outs, counts, sems = refs[: len(spans) * n_ret], refs[-2], refs[-1]
    me = lax.axis_index("ret")
    part = lax.rem(lax.axis_index("ctx"), 2)

    def copy(chunk, k, row, slot):
        source = normed_ref.at[row, part] if spans[chunk][2] else normed_ref.at[row]
        return pltpu.make_async_copy(source, outs[chunk * n_ret + k].at[slot], sems.at[chunk, k, slot])

    for chunk, (start, count, _) in enumerate(spans):
        for k in range(n_ret):

            def send(i, used, k=k, chunk=chunk, start=start):
                request = (start * NEIGHBOURS + i) * 2
                mine = id_ref[k, request] == me

                @pl.when(mine)
                def _():
                    copy(chunk, k, id_ref[k, request + 1], used).start()

                return used + jnp.where(mine, 1, 0)

            counts[chunk, k] = lax.fori_loop(0, count * NEIGHBOURS, send, jnp.int32(0))
    for chunk in range(len(spans)):
        for k in range(n_ret):

            def wait(i, carry, k=k, chunk=chunk):
                copy(chunk, k, 0, i).wait()
                return carry

            lax.fori_loop(0, counts[chunk, k], wait, 0)


def pick(ids, normed, spans, capacity):
    n_ret, width = ids.shape[0], normed.shape[-1]
    slots = [capacity(count) for _, count, _ in spans]
    shapes = [(cap, HALF, width) if pair else (cap, 2, HALF, width) for (_, _, pair), cap in zip(spans, slots)]
    shapes = [jax.ShapeDtypeStruct(shape, BF16) for shape in shapes for _ in range(n_ret)]
    picked = pl.pallas_call(
        functools.partial(pick_kernel, spans),
        in_specs=[SMEM, ANY],
        out_specs=[VMEM] * len(shapes),
        out_shape=shapes,
        scratch_shapes=[
            pltpu.SMEM((len(spans), n_ret), jnp.int32),
            pltpu.SemaphoreType.DMA((len(spans), n_ret, max(slots))),
        ],
        compiler_params=params(16),
        name="pick_rows",
    )(ids, normed)
    return [picked[i : i + n_ret] for i in range(0, len(picked), n_ret)]


def unpack_kernel(start, count, id_ref, *refs):
    *incoming, out_ref, ranks, sems = refs
    me = lax.axis_index("ret")

    def copy(k, rank, i):
        return pltpu.make_async_copy(incoming[k].at[rank], out_ref.at[i], sems.at[i])

    for k in range(len(incoming)):
        ranks[k] = 0
    for i in range(count * NEIGHBOURS):
        source = id_ref[(start * NEIGHBOURS + i) * 2] ^ me
        rank = ranks[source]
        ranks[source] = rank + 1
        for k in range(len(incoming)):

            @pl.when(source == k)
            def _(k=k, rank=rank, i=i):
                copy(k, rank, i).start()

    for i in range(count * NEIGHBOURS):
        copy(0, 0, i).wait()


def unpack(own, incoming, start, count):
    return pl.pallas_call(
        functools.partial(unpack_kernel, start, count),
        in_specs=[SMEM] + [ANY] * len(incoming),
        out_specs=VMEM,
        out_shape=jax.ShapeDtypeStruct((count * NEIGHBOURS,) + incoming[0].shape[1:], BF16),
        scratch_shapes=[
            pltpu.SMEM((len(incoming),), jnp.int32),
            pltpu.SemaphoreType.DMA((count * NEIGHBOURS,)),
        ],
        compiler_params=params(8),
        name="unpack_rows",
    )(own, *incoming)


def block_grads(context, wk_ref, wv_ref, q_ref, go_ref, out_ref, gq_ref, dk_ref, dv_ref):
    scale = 1.0 / math.sqrt(HEAD_DIM)
    keys = jnp.dot(context, wk_ref[...], preferred_element_type=F32).astype(BF16)
    values = jnp.dot(context, wv_ref[...], preferred_element_type=F32).astype(BF16)
    tokens, heads = q_ref.shape[0], q_ref.shape[1] // HEAD_DIM
    zero = jnp.zeros((tokens, HEAD_DIM), BF16)
    cols = [slice(head * HEAD_DIM, (head + 1) * HEAD_DIM) for head in range(heads)]

    def reader(head):
        upper = jnp.concatenate([q_ref[:, cols[head]], zero], axis=1)
        lower = jnp.concatenate([zero, go_ref[:, cols[head]]], axis=1)
        return jnp.concatenate([upper, lower], axis=0)

    def both(head):
        return jnp.concatenate([keys[:, cols[head]], values[:, cols[head]]], axis=1)

    def finish(head, probs, dscore):
        mixed = jnp.dot(jnp.concatenate([probs, dscore], axis=0), both(head), preferred_element_type=F32)
        out_ref[:, cols[head]] = mixed[:tokens, HEAD_DIM:].astype(BF16)
        gq_ref[:, cols[head]] = mixed[tokens:, :HEAD_DIM].astype(BF16)
        grads = contract(jnp.concatenate([dscore, probs], axis=0), reader(head), ((0,), (0,))).astype(BF16)
        dk_ref[:, cols[head]] = grads[:, :HEAD_DIM]
        dv_ref[:, cols[head]] = grads[:, HEAD_DIM:]

    ahead, lag = 3, 2
    products, weights = {}, {}
    for head in range(-ahead, heads + lag):
        if 0 <= head + ahead < heads:
            products[head + ahead] = contract(reader(head + ahead), both(head + ahead), ((1,), (1,)))
        if 0 <= head < heads:
            product = products.pop(head)
            expo, dprob = jnp.exp(product[:tokens] * scale), product[tokens:]
            inverse = 1.0 / jnp.sum(expo, axis=-1, keepdims=True)
            delta = jnp.sum(expo * dprob, axis=-1, keepdims=True) * inverse
            probs = expo * inverse
            weights[head] = (probs.astype(BF16), (probs * (dprob - delta) * scale).astype(BF16))
        if 0 <= head - lag < heads:
            finish(head - lag, *weights.pop(head - lag))


def attend_kernel(first, last, slot_ref, one_ref, two_ref, wk_ref, wv_ref, q_ref, go_ref, *refs):
    refs = list(refs[0 if first else 2 :])
    acc_in = [] if first else [refs.pop(0), refs.pop(0)]
    out_ref, gq_ref, *grad_refs, acck, accv, dk_ref, dv_ref, sems = refs
    accs, grads = (acck, accv), (dk_ref, dv_ref)
    step, steps = pl.program_id(0), pl.num_programs(0)
    loads = [pltpu.make_async_copy(src, dst, sems.at[i]) for i, (src, dst) in enumerate(zip(acc_in, accs))]

    @pl.when(step == 0)
    def _():
        for load in loads:
            load.start()

    width = one_ref.shape[-1]
    context = jnp.concatenate([one_ref[...].reshape(-1, width), two_ref[...].reshape(-1, width)], axis=0)
    block_grads(context, wk_ref, wv_ref, q_ref, go_ref, out_ref, gq_ref, dk_ref, dv_ref)

    @pl.when(step == 0)
    def _():
        for load in loads:
            load.wait()
        if first:
            for acc, grad in zip(accs, grads):
                acc[...] = contract(context, grad[...], ((0,), (0,)))

    @pl.when((step > 0) | (not first))
    def _():
        for acc, grad in zip(accs, grads):
            acc[...] += contract(context, grad[...], ((0,), (0,)))

    @pl.when(step == steps - 1)
    def _():
        if last:
            half = grad_refs[0].shape[0]
            dp = lax.axis_index("dp")
            for i, side in enumerate((1 - dp, dp)):
                for acc, grad_ref in zip(accs, grad_refs[2 * i : 2 * i + 2]):
                    grad_ref[...] = acc[pl.ds(pl.multiple_of(side * half, half), half), :].astype(BF16)
        else:
            stores = [pltpu.make_async_copy(acc, dst, sems.at[i]) for i, (acc, dst) in enumerate(zip(accs, grad_refs))]
            for store in stores:
                store.start()
            for store in stores:
                store.wait()


def attend(rows, slots, wk, wv, queries, grad_out, start, count, carried, last):
    blocks = slots.shape[0] // (2 * NEIGHBOURS)
    tokens, feat = queries.shape[0] // blocks, queries.shape[1]
    enc = wk.shape[0]
    whole = lambda shape: pl.BlockSpec(shape, lambda b, s: (0, 0))
    row = pl.BlockSpec((tokens, feat), lambda b, s: (start + b, 0))
    if len(rows) == 2:
        neighs = [pl.BlockSpec((NEIGHBOURS, HALF, enc), lambda b, s: (b, 0, 0))] * 2
    else:
        rows = rows * 2
        neighs = [pl.BlockSpec((1, 2, HALF, enc), lambda b, s, n=n: (b * NEIGHBOURS + n, 0, 0, 0)) for n in range(NEIGHBOURS)]
    row_shape = jax.ShapeDtypeStruct(queries.shape, BF16)
    if last:
        grad_shapes = [jax.ShapeDtypeStruct((enc // 2, feat), BF16)] * 4
        grad_specs = [whole((enc // 2, feat))] * 4
    else:
        grad_shapes = [jax.ShapeDtypeStruct((enc, feat), F32)] * 2
        grad_specs = [HBM] * 2
    return pl.pallas_call(
        functools.partial(attend_kernel, not carried, last),
        grid_spec=pltpu.PrefetchScalarGridSpec(
            num_scalar_prefetch=1,
            grid=(count,),
            in_specs=neighs + [whole((enc, feat))] * 2 + [row] * 2 + [HBM] * len(carried),
            out_specs=[row, row] + grad_specs,
            scratch_shapes=[
                pltpu.VMEM((enc, feat), F32),
                pltpu.VMEM((enc, feat), F32),
                pltpu.VMEM((NEIGHBOURS * NEIGH_LEN, feat), BF16),
                pltpu.VMEM((NEIGHBOURS * NEIGH_LEN, feat), BF16),
                pltpu.SemaphoreType.DMA((2,)),
            ],
        ),
        out_shape=[row_shape, row_shape] + grad_shapes,
        input_output_aliases={7: 0, 8: 1} if carried else {},
        compiler_params=params(ATTEND_MIB),
        name="attend_blocks",
    )(slots, *rows, wk, wv, queries, grad_out, *carried)


def fold_kernel(dims, count, *refs):
    ret = lax.axis_index("ret")
    for i in range(count):
        held_ref, arrived_ref = refs[i], refs[count + i]
        if dims is None:
            refs[2 * count + i][...] = held_ref[0].astype(F32) + arrived_ref[0].astype(F32)
            continue
        bit, place = dims[i]
        mine = (ret >> bit) & 1
        stride = 1 << place
        for j in range(held_ref.shape[0] // 2):
            base = (j // stride) * 2 * stride + j % stride
            for k, side in enumerate((1 - mine, mine)):
                row = base + side * stride
                total = held_ref[row].astype(F32) + arrived_ref[row].astype(F32)
                refs[(2 + k) * count + i][j] = total.astype(BF16)


def fold(held, arrived, dims):
    count = len(held)
    parts, rows, feat = held[0].shape
    if dims is None:
        shapes = [jax.ShapeDtypeStruct((rows, feat), F32)] * count
    else:
        shapes = [jax.ShapeDtypeStruct((parts // 2, rows, feat), BF16)] * (2 * count)
    return pl.pallas_call(
        functools.partial(fold_kernel, dims, count),
        in_specs=[VMEM] * (2 * count),
        out_specs=[VMEM] * len(shapes),
        out_shape=shapes,
        compiler_params=params(16),
        name="fold_grads",
    )(*held, *arrived)


def reduce_scatter(send, held):
    n_ret = lax.axis_size("ret")
    bits = n_ret.bit_length() - 1
    arrived = [swap(grad, "dp", 1) for grad in send]
    split = lambda grad: grad.reshape(n_ret, -1, grad.shape[-1])
    held, arrived = [split(grad) for grad in held], [split(grad) for grad in arrived]
    left = [list(range(bits)) for _ in held]
    for step in range(bits):
        bit = [step, bits - 1 - step]
        dims = tuple((b, bits_left.index(b)) for b, bits_left in zip(bit, left))
        *send, held0, held1 = fold(held, arrived, dims)
        held = [held0, held1]
        for b, bits_left in zip(bit, left):
            bits_left.remove(b)
        arrived = [swap(grad, "ret", 1 << b) for grad, b in zip(send, bit)]
    return fold(held, arrived, None)


def spans_of(blocks):
    spans, start = [], 0
    for count, pair in CHUNKS:
        spans.append((start, count, pair))
        start += count
    return spans if start == blocks else [(0, blocks, False)]


def local(queries, enc_states, w_key, w_value, shard_ids, row_ids, grad_out):
    n_ret = lax.axis_size("ret")
    blocks = shard_ids.shape[1]
    bound = blocks * NEIGHBOURS * 2 // n_ret
    enc = enc_states.shape[2]

    def capacity(count):
        return min(count, bound)

    own = jnp.stack([shard_ids[0], row_ids[0]], axis=-1).reshape(-1)
    ids = exchange_ids(own)
    normed = normalize_rows(enc_states[0]).reshape(-1, 2, HALF, enc)
    spans = spans_of(blocks)
    outgoing = pick(ids, normed, spans[:1], capacity)
    if len(spans) > 1:
        outgoing = outgoing + pick(ids, normed, spans[1:], capacity)
    carried, arrivals = [], []
    for slots in outgoing:
        slots = list(slots)
        if arrivals:
            for k in range(1, n_ret):
                arrivals[-1][k], slots[k] = lax.optimization_barrier((arrivals[-1][k], slots[k]))
        arrivals.append(slots[:1] + [swap(slots[k], "ret", k) for k in range(1, n_ret)])
    for incoming, (start, count, pair) in zip(arrivals, spans):
        mine = unpack(own, incoming, start, count)
        rows = [mine, swap(mine, "ctx", 1)] if pair else [mine]
        last = start + count == blocks
        carried = attend(rows, own, w_key, w_value, queries[0], grad_out[0], start, count, carried, last)
    attended, grad_queries, *grads = carried
    grad_w_key, grad_w_value = reduce_scatter(grads[:2], grads[2:])
    return attended[None], grad_queries[None], grad_w_key, grad_w_value


def solution(mesh):
    placed = (
        P("dp", "ret", "ctx"),
        P("dp", "ret", None),
        P(None, "ctx"),
        P(None, "ctx"),
        P("dp", "ret", None),
        P("dp", "ret", None),
        P("dp", "ret", "ctx"),
    )
    return jax.shard_map(
        local,
        mesh=mesh,
        in_specs=placed,
        out_specs=(
            P("dp", "ret", "ctx"),
            P("dp", "ret", "ctx"),
            P(("dp", "ret"), "ctx"),
            P(("dp", "ret"), "ctx"),
        ),
        check_vma=False,
    )
```

```python
import functools
import math

import jax
import jax.numpy as jnp
from jax import lax
from jax.experimental import pallas as pl
from jax.experimental.pallas import tpu as pltpu
from jax.sharding import PartitionSpec as P

HEAD_DIM = 128
NEIGH_LEN = 128
NEIGHBOURS = 2
HALF = NEIGH_LEN // 2
MIB = 1024 * 1024
ATTEND_MIB = 26
WEIGH_MIB = 26
PIECES = 2
CHUNKS = ((3, True), (3, True), (2, False))

F32 = jnp.float32
BF16 = jnp.bfloat16
ANY = pl.BlockSpec(memory_space=pl.ANY)
SMEM = pl.BlockSpec(memory_space=pltpu.SMEM)
VMEM = pl.BlockSpec(memory_space=pltpu.VMEM)
HBM = pl.BlockSpec(memory_space=pltpu.HBM)


def params(mib):
    return pltpu.CompilerParams(vmem_limit_bytes=mib * MIB)


def contract(lhs, rhs, dims):
    return lax.dot_general(lhs, rhs, (dims, ((), ())), preferred_element_type=F32)


def swap(array, axis, bit):
    size = lax.axis_size(axis)
    return lax.ppermute(array, axis, [(i, i ^ bit) for i in range(size)])


def normalize_kernel(states_ref, out_ref):
    floats = states_ref[...].astype(F32)
    mean_square = jnp.mean(floats * floats, axis=-1, keepdims=True)
    out_ref[...] = (floats * lax.rsqrt(mean_square + 1e-06)).astype(BF16)


def normalize_rows(states):
    rows, width = states.shape
    tile = 512
    spec = pl.BlockSpec((tile, width), lambda i: (i, 0))
    return pl.pallas_call(
        normalize_kernel,
        grid=(rows // tile,),
        in_specs=[spec],
        out_specs=spec,
        out_shape=jax.ShapeDtypeStruct(states.shape, BF16),
        compiler_params=params(12),
        name="normalize_rows",
    )(states)


def exchange_ids(own):
    n_ret = lax.axis_size("ret")
    if n_ret <= 4:
        return jnp.stack([own] + [swap(own, "ret", k) for k in range(1, n_ret)])
    every = lax.all_gather(own, "ret")
    order = jnp.arange(n_ret, dtype=jnp.int32) ^ lax.axis_index("ret")
    return jnp.take(every, order, axis=0)


def pick_kernel(spans, id_ref, normed_ref, *refs):
    n_ret = id_ref.shape[0]
    outs, counts, sems = refs[: len(spans) * n_ret], refs[-2], refs[-1]
    me = lax.axis_index("ret")
    part = lax.rem(lax.axis_index("ctx"), 2)

    def copy(chunk, k, row, slot):
        source = normed_ref.at[row, part] if spans[chunk][2] else normed_ref.at[row]
        return pltpu.make_async_copy(source, outs[chunk * n_ret + k].at[slot], sems.at[chunk, k, slot])

    for chunk, (start, count, _) in enumerate(spans):
        for k in range(n_ret):

            def send(i, used, k=k, chunk=chunk, start=start):
                request = (start * NEIGHBOURS + i) * 2
                mine = id_ref[k, request] == me

                @pl.when(mine)
                def _():
                    copy(chunk, k, id_ref[k, request + 1], used).start()

                return used + jnp.where(mine, 1, 0)

            counts[chunk, k] = lax.fori_loop(0, count * NEIGHBOURS, send, jnp.int32(0))
    for chunk in range(len(spans)):
        for k in range(n_ret):

            def wait(i, carry, k=k, chunk=chunk):
                copy(chunk, k, 0, i).wait()
                return carry

            lax.fori_loop(0, counts[chunk, k], wait, 0)


def pick(ids, normed, spans, capacity):
    n_ret, width = ids.shape[0], normed.shape[-1]
    slots = [capacity(count) for _, count, _ in spans]
    shapes = [(cap, HALF, width) if pair else (cap, 2, HALF, width) for (_, _, pair), cap in zip(spans, slots)]
    shapes = [jax.ShapeDtypeStruct(shape, BF16) for shape in shapes for _ in range(n_ret)]
    picked = pl.pallas_call(
        functools.partial(pick_kernel, spans),
        in_specs=[SMEM, ANY],
        out_specs=[VMEM] * len(shapes),
        out_shape=shapes,
        scratch_shapes=[
            pltpu.SMEM((len(spans), n_ret), jnp.int32),
            pltpu.SemaphoreType.DMA((len(spans), n_ret, max(slots))),
        ],
        compiler_params=params(16),
        name="pick_rows",
    )(ids, normed)
    return [picked[i : i + n_ret] for i in range(0, len(picked), n_ret)]


def unpack_kernel(start, count, id_ref, *refs):
    *incoming, out_ref, ranks, sems = refs
    me = lax.axis_index("ret")

    def copy(k, rank, i):
        return pltpu.make_async_copy(incoming[k].at[rank], out_ref.at[i], sems.at[i])

    for k in range(len(incoming)):
        ranks[k] = 0
    for i in range(count * NEIGHBOURS):
        source = id_ref[(start * NEIGHBOURS + i) * 2] ^ me
        rank = ranks[source]
        ranks[source] = rank + 1
        for k in range(len(incoming)):

            @pl.when(source == k)
            def _(k=k, rank=rank, i=i):
                copy(k, rank, i).start()

    for i in range(count * NEIGHBOURS):
        copy(0, 0, i).wait()


def unpack(own, incoming, start, count):
    return pl.pallas_call(
        functools.partial(unpack_kernel, start, count),
        in_specs=[SMEM] + [ANY] * len(incoming),
        out_specs=VMEM,
        out_shape=jax.ShapeDtypeStruct((count * NEIGHBOURS,) + incoming[0].shape[1:], BF16),
        scratch_shapes=[
            pltpu.SMEM((len(incoming),), jnp.int32),
            pltpu.SemaphoreType.DMA((count * NEIGHBOURS,)),
        ],
        compiler_params=params(8),
        name="unpack_rows",
    )(own, *incoming)


def block_grads(keys, values, query, grad, out_ref, gq_ref, dk_ref, dv_ref):
    scale = 1.0 / math.sqrt(HEAD_DIM)
    tokens, heads = out_ref.shape[0], out_ref.shape[1] // HEAD_DIM
    zero = jnp.zeros((tokens, HEAD_DIM), BF16)
    cols = [slice(head * HEAD_DIM, (head + 1) * HEAD_DIM) for head in range(heads)]

    def reader(head):
        upper = jnp.concatenate([query(cols[head]), zero], axis=1)
        lower = jnp.concatenate([zero, grad(cols[head])], axis=1)
        return jnp.concatenate([upper, lower], axis=0)

    def both(head):
        return jnp.concatenate([keys(cols[head]), values(cols[head])], axis=1)

    def finish(head, probs, dscore):
        mixed = jnp.dot(jnp.concatenate([probs, dscore], axis=0), both(head), preferred_element_type=F32)
        out_ref[:, cols[head]] = mixed[:tokens, HEAD_DIM:].astype(BF16)
        gq_ref[:, cols[head]] = mixed[tokens:, :HEAD_DIM].astype(BF16)
        grads = contract(jnp.concatenate([dscore, probs], axis=0), reader(head), ((0,), (0,))).astype(BF16)
        dk_ref[:, cols[head]] = grads[:, :HEAD_DIM]
        dv_ref[:, cols[head]] = grads[:, HEAD_DIM:]

    ahead, lag = 3, 2
    products, weights = {}, {}
    for head in range(-ahead, heads + lag):
        if 0 <= head + ahead < heads:
            products[head + ahead] = contract(reader(head + ahead), both(head + ahead), ((1,), (1,)))
        if 0 <= head < heads:
            product = products.pop(head)
            expo, dprob = jnp.exp(product[:tokens] * scale), product[tokens:]
            inverse = 1.0 / jnp.sum(expo, axis=-1, keepdims=True)
            delta = jnp.sum(expo * dprob, axis=-1, keepdims=True) * inverse
            probs = expo * inverse
            weights[head] = (probs.astype(BF16), (probs * (dprob - delta) * scale).astype(BF16))
        if 0 <= head - lag < heads:
            finish(head - lag, *weights.pop(head - lag))


def attend_kernel(start, count, direct, first, id_ref, *refs):
    refs = list(refs)
    take = lambda n: [refs.pop(0) for _ in range(n)]
    row_refs = take(direct if direct else 2)
    wk_ref, wv_ref, q_in, go_in = take(4)
    take(0 if first else 2)
    out_hbm, gq_hbm, turned = take(3)
    grad_refs = take(2 * PIECES)
    q_ref, go_ref, out_ref, gq_ref, keys, values, dk_ref, dv_ref, rows, sems, row_sems, ranks = take(12)
    size, width = rows.shape[1:]
    feat = keys.shape[2]
    blocks = pl.ds(start, count)

    ins = [pltpu.make_async_copy(src.at[blocks], dst, sems.at[i]) for i, (src, dst) in enumerate(((q_in, q_ref), (go_in, go_ref)))]
    if direct:
        me = lax.axis_index("ret")

        def fetch(k, rank, i):
            b, n = divmod(i, NEIGHBOURS)
            return pltpu.make_async_copy(row_refs[k].at[rank], rows.at[b, pl.ds(n * NEIGH_LEN, NEIGH_LEN)], row_sems.at[i])

        for k in range(direct):
            ranks[k] = 0
        for i in range(count * NEIGHBOURS):
            source = id_ref[(start * NEIGHBOURS + i) * 2] ^ me
            rank = ranks[source]
            ranks[source] = rank + 1
            for k in range(direct):

                @pl.when(source == k)
                def _(k=k, rank=rank, i=i):
                    fetch(k, rank, i).start()

        for copy in ins:
            copy.start()
        for i in range(count * NEIGHBOURS):
            fetch(0, 0, i).wait()
    else:
        for copy in ins:
            copy.start()
        part = size // 2
        for i, ref in enumerate(row_refs):
            rows[:, i * part : (i + 1) * part] = ref[...].reshape(count, part, width)

    every = rows[...].reshape(-1, width)
    turned[...] = every.T
    for w_ref, target in ((wk_ref, keys), (wv_ref, values)):
        product = jnp.dot(every, w_ref[...], preferred_element_type=F32).astype(BF16)
        target[...] = product.reshape(count, size, feat)
    for copy in ins:
        copy.wait()

    def block(b, carry):
        pick = lambda ref: lambda cols: ref[b, :, cols]
        block_grads(pick(keys), pick(values), pick(q_ref), pick(go_ref), out_ref.at[b], gq_ref.at[b], dk_ref.at[b], dv_ref.at[b])
        return carry

    lax.fori_loop(0, count, block, 0)
    outs = [pltpu.make_async_copy(src, dst.at[blocks], sems.at[i]) for i, (src, dst) in enumerate(((out_ref, out_hbm), (gq_ref, gq_hbm)))]
    for copy in outs:
        copy.start()
    span = feat // PIECES
    for piece in range(PIECES):
        cols = slice(piece * span, (piece + 1) * span)
        for i, grad in enumerate((dk_ref, dv_ref)):
            grad_refs[2 * piece + i][...] = grad[:, :, cols].reshape(-1, span)
    for copy in outs:
        copy.wait()


def attend(rows, own, wk, wv, queries, grad_out, start, count, carried):
    _, tokens, feat = queries.shape
    enc = wk.shape[0]
    context = NEIGHBOURS * NEIGH_LEN
    direct = 0 if len(rows) == 2 else len(rows)
    row_shape = jax.ShapeDtypeStruct(queries.shape, BF16)
    if direct:
        rows = [part.reshape(part.shape[0], NEIGH_LEN, enc) for part in rows]
    turned_shape = jax.ShapeDtypeStruct((enc, count * context), BF16)
    grad_shapes = [jax.ShapeDtypeStruct((count * context, feat // PIECES), BF16)] * (2 * PIECES)
    aliased = 1 + len(rows) + 4
    return pl.pallas_call(
        functools.partial(attend_kernel, start, count, direct, not carried),
        in_specs=[SMEM] + [ANY if direct else VMEM] * len(rows) + [VMEM] * 2 + [HBM] * 2 + [HBM] * len(carried),
        out_specs=[HBM] * 2 + [VMEM] * (1 + 2 * PIECES),
        scratch_shapes=[
            pltpu.VMEM((count, tokens, feat), BF16),
            pltpu.VMEM((count, tokens, feat), BF16),
            pltpu.VMEM((count, tokens, feat), BF16),
            pltpu.VMEM((count, tokens, feat), BF16),
            pltpu.VMEM((count, context, feat), BF16),
            pltpu.VMEM((count, context, feat), BF16),
            pltpu.VMEM((count, context, feat), BF16),
            pltpu.VMEM((count, context, feat), BF16),
            pltpu.VMEM((count, context, enc), BF16),
            pltpu.SemaphoreType.DMA((2,)),
            pltpu.SemaphoreType.DMA((count * NEIGHBOURS,)),
            pltpu.SMEM((max(direct, 1),), jnp.int32),
        ],
        out_shape=[row_shape, row_shape, turned_shape] + grad_shapes,
        input_output_aliases={aliased: 0, aliased + 1: 1} if carried else {},
        compiler_params=params(ATTEND_MIB),
        name="attend_blocks",
    )(own, *rows, wk, wv, queries, grad_out, *carried)


def weigh_kernel(chunks, *refs):
    half = refs[0].shape[0] // 2
    dp = lax.axis_index("dp")
    for i in range(2):
        total = 0.0
        for c in range(chunks):
            total += jnp.dot(refs[c][...], refs[(1 + i) * chunks + c][...], preferred_element_type=F32)
        refs[-1][...] = total
        for j, side in enumerate((1 - dp, dp)):
            refs[3 * chunks + 2 * j + i][...] = refs[-1][pl.ds(pl.multiple_of(side * half, half), half), :].astype(BF16)


def weigh(turned, dks, dvs):
    enc, width = turned[0].shape[0], dks[0].shape[1]
    return pl.pallas_call(
        functools.partial(weigh_kernel, len(turned)),
        in_specs=[VMEM] * (3 * len(turned)),
        out_specs=[VMEM] * 4,
        out_shape=[jax.ShapeDtypeStruct((enc // 2, width), BF16)] * 4,
        scratch_shapes=[pltpu.VMEM((enc, width), F32)],
        compiler_params=params(WEIGH_MIB),
        name="weigh_grads",
    )(*turned, *dks, *dvs)


def fold_kernel(dims, count, *refs):
    ret = lax.axis_index("ret")
    for i in range(count):
        held_ref, arrived_ref = refs[i], refs[count + i]
        bit, place = dims[i]
        mine = (ret >> bit) & 1
        stride = 1 << place
        for j in range(held_ref.shape[0] // 2):
            base = (j // stride) * 2 * stride + j % stride
            for k, side in enumerate((1 - mine, mine)):
                row = base + side * stride
                total = held_ref[row].astype(F32) + arrived_ref[row].astype(F32)
                refs[(2 + k) * count + i][j] = total.astype(BF16)


def fold(held, arrived, dims):
    count = len(held)
    parts, rows, width = held[0].shape
    shapes = [jax.ShapeDtypeStruct((parts // 2, rows, width), BF16)] * (2 * count)
    return pl.pallas_call(
        functools.partial(fold_kernel, dims, count),
        in_specs=[VMEM] * (2 * count),
        out_specs=[VMEM] * len(shapes),
        out_shape=shapes,
        compiler_params=params(16),
        name="fold_grads",
    )(*held, *arrived)


def join_kernel(*refs):
    count = (len(refs) - 2) // 2
    for i in range(count):
        total = refs[i][0].astype(F32) + refs[count + i][0].astype(F32)
        width = total.shape[1]
        refs[2 * count + i % 2][:, i // 2 * width : (i // 2 + 1) * width] = total


def join(held, arrived):
    _, rows, width = held[0].shape
    return pl.pallas_call(
        join_kernel,
        in_specs=[VMEM] * (2 * len(held)),
        out_specs=[VMEM] * 2,
        out_shape=[jax.ShapeDtypeStruct((rows, len(held) // 2 * width), F32)] * 2,
        compiler_params=params(16),
        name="join_grads",
    )(*held, *arrived)


def reduce_scatter(send, held):
    n_ret = lax.axis_size("ret")
    bits = n_ret.bit_length() - 1
    arrived = [swap(grad, "dp", 1) for grad in send]
    split = lambda grad: grad.reshape(n_ret, -1, grad.shape[-1])
    held, arrived = [split(grad) for grad in held], [split(grad) for grad in arrived]
    left = [list(range(bits)) for _ in range(2)]
    for step in range(bits):
        bit = [step, bits - 1 - step]
        dims = tuple((b, bits_left.index(b)) for b, bits_left in zip(bit, left))
        for b, bits_left in zip(bit, left):
            bits_left.remove(b)
        for piece in range(0, len(held), 2):
            pair = slice(piece, piece + 2)
            parts = fold(held[pair], arrived[pair], dims)
            held[pair] = parts[2:]
            arrived[pair] = [swap(grad, "ret", 1 << b) for grad, b in zip(parts[:2], bit)]
    return join(held, arrived)


def spans_of(blocks):
    spans, start = [], 0
    for count, pair in CHUNKS:
        spans.append((start, count, pair))
        start += count
    return spans if start == blocks else [(0, blocks, False)]


def local(queries, enc_states, w_key, w_value, shard_ids, row_ids, grad_out):
    n_ret = lax.axis_size("ret")
    blocks = shard_ids.shape[1]
    bound = blocks * NEIGHBOURS * 2 // n_ret
    enc = enc_states.shape[2]

    def capacity(count):
        return min(count, bound)

    own = jnp.stack([shard_ids[0], row_ids[0]], axis=-1).reshape(-1)
    ids = exchange_ids(own)
    normed = normalize_rows(enc_states[0]).reshape(-1, 2, HALF, enc)
    spans = spans_of(blocks)
    outgoing = pick(ids, normed, spans[:1], capacity)
    if len(spans) > 1:
        outgoing = outgoing + pick(ids, normed, spans[1:], capacity)
    query_blocks, grad_blocks = (array.reshape(blocks, -1, array.shape[2]) for array in (queries, grad_out))
    carried, arrivals = [], []
    for slots in outgoing:
        slots = list(slots)
        if arrivals:
            for k in range(1, n_ret):
                arrivals[-1][k], slots[k] = lax.optimization_barrier((arrivals[-1][k], slots[k]))
        arrivals.append(slots[:1] + [swap(slots[k], "ret", k) for k in range(1, n_ret)])
    rows, turned, found = [None] * len(spans), [], []

    def prepare(i):
        start, count, pair = spans[i]
        if pair:
            mine = unpack(own, arrivals[i], start, count)
            rows[i] = [mine, swap(mine, "ctx", 1)]
        else:
            rows[i] = arrivals[i]

    prepare(0)
    for i, (start, count, pair) in enumerate(spans):
        last = i + 1 == len(spans)
        if not last and spans[i + 1][2]:
            prepare(i + 1)
            rows[i][0], rows[i + 1][0] = lax.optimization_barrier((rows[i][0], rows[i + 1][0]))
        attended, grad_queries, flipped, *grads = attend(rows[i], own, w_key, w_value, query_blocks, grad_blocks, start, count, carried)
        carried = [attended, grad_queries]
        turned.append(flipped)
        found.append(grads)
        if not last and rows[i + 1] is None:
            carried[0], arrivals[i + 1] = lax.optimization_barrier((carried[0], arrivals[i + 1]))
            prepare(i + 1)
    send, held = [], []
    for piece in range(PIECES):
        parts = weigh(turned, *([grads[2 * piece + i] for grads in found] for i in range(2)))
        send += parts[:2]
        held += parts[2:]
    attended, grad_queries = carried
    grad_w_key, grad_w_value = reduce_scatter(send, held)
    return attended.reshape(queries.shape), grad_queries.reshape(queries.shape), grad_w_key, grad_w_value


def solution(mesh):
    placed = (
        P("dp", "ret", "ctx"),
        P("dp", "ret", None),
        P(None, "ctx"),
        P(None, "ctx"),
        P("dp", "ret", None),
        P("dp", "ret", None),
        P("dp", "ret", "ctx"),
    )
    return jax.shard_map(
        local,
        mesh=mesh,
        in_specs=placed,
        out_specs=(
            P("dp", "ret", "ctx"),
            P("dp", "ret", "ctx"),
            P(("dp", "ret"), "ctx"),
            P(("dp", "ret"), "ctx"),
        ),
        check_vma=False,
    )
```

```python
import functools
import math

import jax
import jax.numpy as jnp
from jax import lax
from jax.experimental import pallas as pl
from jax.experimental.pallas import tpu as pltpu
from jax.sharding import PartitionSpec as P

HEAD_DIM = 128
NEIGH_LEN = 128
NEIGHBOURS = 2
HALF = NEIGH_LEN // 2
MIB = 1024 * 1024
ATTEND_MIB = 26
WEIGH_MIB = 26
PIECES = 2
FIRST_PIECE = 6 / 8
CHUNKS = ((3, True), (3, True), (2, False))

F32 = jnp.float32
BF16 = jnp.bfloat16
ANY = pl.BlockSpec(memory_space=pl.ANY)
SMEM = pl.BlockSpec(memory_space=pltpu.SMEM)
VMEM = pl.BlockSpec(memory_space=pltpu.VMEM)
HBM = pl.BlockSpec(memory_space=pltpu.HBM)


def params(mib):
    return pltpu.CompilerParams(vmem_limit_bytes=mib * MIB)


def piece_heads(heads):
    return [0, int(heads * FIRST_PIECE), heads]


def contract(lhs, rhs, dims):
    return lax.dot_general(lhs, rhs, (dims, ((), ())), preferred_element_type=F32)


def swap(array, axis, bit):
    size = lax.axis_size(axis)
    return lax.ppermute(array, axis, [(i, i ^ bit) for i in range(size)])


def normalize_kernel(states_ref, out_ref):
    floats = states_ref[...].astype(F32)
    mean_square = jnp.mean(floats * floats, axis=-1, keepdims=True)
    out_ref[...] = (floats * lax.rsqrt(mean_square + 1e-06)).astype(BF16)


def normalize_rows(states):
    rows, width = states.shape
    tile = 512
    spec = pl.BlockSpec((tile, width), lambda i: (i, 0))
    return pl.pallas_call(
        normalize_kernel,
        grid=(rows // tile,),
        in_specs=[spec],
        out_specs=spec,
        out_shape=jax.ShapeDtypeStruct(states.shape, BF16),
        compiler_params=params(12),
        name="normalize_rows",
    )(states)


def exchange_ids(own):
    n_ret = lax.axis_size("ret")
    if n_ret <= 4:
        return jnp.stack([own] + [swap(own, "ret", k) for k in range(1, n_ret)])
    every = lax.all_gather(own, "ret")
    order = jnp.arange(n_ret, dtype=jnp.int32) ^ lax.axis_index("ret")
    return jnp.take(every, order, axis=0)


def pick_kernel(spans, id_ref, normed_ref, *outs):
    n_ret = id_ref.shape[0]
    me = lax.axis_index("ret")
    part = lax.rem(lax.axis_index("ctx"), 2)
    for chunk, (start, count, pair) in enumerate(spans):
        for k in range(n_ret):
            out_ref = outs[chunk * n_ret + k]

            def send(i, used, k=k, start=start, pair=pair, out_ref=out_ref):
                request = (start * NEIGHBOURS + i) * 2
                mine = id_ref[k, request] == me

                @pl.when(mine)
                def _():
                    row = id_ref[k, request + 1]
                    out_ref[used] = normed_ref[row, part] if pair else normed_ref[row]

                return used + jnp.where(mine, 1, 0)

            lax.fori_loop(0, count * NEIGHBOURS, send, jnp.int32(0))


def pick(ids, normed, spans, capacity):
    n_ret, width = ids.shape[0], normed.shape[-1]
    slots = [capacity(count) for _, count, _ in spans]
    shapes = [(cap, HALF, width) if pair else (cap, 2, HALF, width) for (_, _, pair), cap in zip(spans, slots)]
    shapes = [jax.ShapeDtypeStruct(shape, BF16) for shape in shapes for _ in range(n_ret)]
    picked = pl.pallas_call(
        functools.partial(pick_kernel, spans),
        in_specs=[SMEM, VMEM],
        out_specs=[VMEM] * len(shapes),
        out_shape=shapes,
        compiler_params=params(16),
        name="pick_rows",
    )(ids, normed)
    return [picked[i : i + n_ret] for i in range(0, len(picked), n_ret)]


def unpack_kernel(start, count, id_ref, *refs):
    *incoming, out_ref, ranks = refs
    place_rows(start, count, id_ref, incoming, ranks, lambda i: out_ref.at[i])


def place_rows(start, count, id_ref, incoming, ranks, target):
    me = lax.axis_index("ret")
    for k in range(len(incoming)):
        ranks[k] = 0
    for i in range(count * NEIGHBOURS):
        source = id_ref[(start * NEIGHBOURS + i) * 2] ^ me
        rank = ranks[source]
        ranks[source] = rank + 1
        for k in range(len(incoming)):

            @pl.when(source == k)
            def _(k=k, rank=rank, i=i):
                target(i)[...] = incoming[k][rank]


def unpack(own, incoming, start, count):
    return pl.pallas_call(
        functools.partial(unpack_kernel, start, count),
        in_specs=[SMEM] + [VMEM] * len(incoming),
        out_specs=VMEM,
        out_shape=jax.ShapeDtypeStruct((count * NEIGHBOURS,) + incoming[0].shape[1:], BF16),
        scratch_shapes=[pltpu.SMEM((len(incoming),), jnp.int32)],
        compiler_params=params(8),
        name="unpack_rows",
    )(own, *incoming)


def block_grads(keys, values, query, grad, out_ref, gq_ref, grad_refs):
    scale = 1.0 / math.sqrt(HEAD_DIM)
    tokens, heads = out_ref.shape[0], out_ref.shape[1] // HEAD_DIM
    zero = jnp.zeros((tokens, HEAD_DIM), BF16)
    bounds = piece_heads(heads)
    cols = [slice(head * HEAD_DIM, (head + 1) * HEAD_DIM) for head in range(heads)]

    def reader(head):
        upper = jnp.concatenate([query(cols[head]), zero], axis=1)
        lower = jnp.concatenate([zero, grad(cols[head])], axis=1)
        return jnp.concatenate([upper, lower], axis=0)

    def both(head):
        return jnp.concatenate([keys(cols[head]), values(cols[head])], axis=1)

    def finish(head, probs, dscore):
        mixed = jnp.dot(jnp.concatenate([probs, dscore], axis=0), both(head), preferred_element_type=F32)
        out_ref[:, cols[head]] = mixed[:tokens, HEAD_DIM:].astype(BF16)
        gq_ref[:, cols[head]] = mixed[tokens:, :HEAD_DIM].astype(BF16)
        grads = contract(jnp.concatenate([dscore, probs], axis=0), reader(head), ((0,), (0,))).astype(BF16)
        piece = int(head >= bounds[1])
        place = cols[head - bounds[piece]]
        grad_refs[2 * piece][:, place] = grads[:, :HEAD_DIM]
        grad_refs[2 * piece + 1][:, place] = grads[:, HEAD_DIM:]

    ahead, lag = 3, 2
    products, weights = {}, {}
    for head in range(-ahead, heads + lag):
        if 0 <= head + ahead < heads:
            products[head + ahead] = contract(reader(head + ahead), both(head + ahead), ((1,), (1,)))
        if 0 <= head < heads:
            product = products.pop(head)
            expo, dprob = jnp.exp(product[:tokens] * scale), product[tokens:]
            inverse = 1.0 / jnp.sum(expo, axis=-1, keepdims=True)
            delta = jnp.sum(expo * dprob, axis=-1, keepdims=True) * inverse
            probs = expo * inverse
            weights[head] = (probs.astype(BF16), (probs * (dprob - delta) * scale).astype(BF16))
        if 0 <= head - lag < heads:
            finish(head - lag, *weights.pop(head - lag))


def attend_kernel(start, count, direct, first, id_ref, *refs):
    refs = list(refs)
    take = lambda n: [refs.pop(0) for _ in range(n)]
    row_refs = take(direct if direct else 2)
    wk_ref, wv_ref, q_ref, go_ref = take(4)
    take(0 if first else 2)
    out_hbm, gq_hbm, turned = take(3)
    grad_refs = take(2 * PIECES)
    out_ref, gq_ref, keys, values, rows, sems, ranks = take(7)
    size, width = rows.shape[1:]
    feat = keys.shape[2]
    if direct:
        place_rows(start, count, id_ref, row_refs, ranks, lambda i: rows.at[i // NEIGHBOURS, pl.ds(i % NEIGHBOURS * NEIGH_LEN, NEIGH_LEN)])
    else:
        part = size // 2
        for i, ref in enumerate(row_refs):
            rows[:, i * part : (i + 1) * part] = ref[...].reshape(count, part, width)

    every = rows[...].reshape(-1, width)
    turned[...] = every.T
    for w_ref, target in ((wk_ref, keys), (wv_ref, values)):
        product = jnp.dot(every, w_ref[...], preferred_element_type=F32).astype(BF16)
        target[...] = product.reshape(count, size, feat)

    def stores(b):
        pairs = ((out_ref, out_hbm), (gq_ref, gq_hbm))
        return [pltpu.make_async_copy(src.at[b], dst.at[start + b], sems.at[b, i]) for i, (src, dst) in enumerate(pairs)]

    def block(b, carry):
        pick = lambda ref, at: lambda cols: ref[at, :, cols]
        inputs = pick(keys, b), pick(values, b), pick(q_ref, start + b), pick(go_ref, start + b)
        block_grads(*inputs, out_ref.at[b], gq_ref.at[b], [ref.at[b] for ref in grad_refs])
        for store in stores(b):
            store.start()
        return carry

    lax.fori_loop(0, count, block, 0)
    for b in range(count):
        for store in stores(b):
            store.wait()


def attend(rows, own, wk, wv, queries, grad_out, start, count, carried):
    _, tokens, feat = queries.shape
    enc = wk.shape[0]
    context = NEIGHBOURS * NEIGH_LEN
    direct = 0 if len(rows) == 2 else len(rows)
    row_shape = jax.ShapeDtypeStruct(queries.shape, BF16)
    if direct:
        rows = [part.reshape(part.shape[0], NEIGH_LEN, enc) for part in rows]
    turned_shape = jax.ShapeDtypeStruct((enc, count * context), BF16)
    bounds = piece_heads(feat // HEAD_DIM)
    widths = [(bounds[piece + 1] - bounds[piece]) * HEAD_DIM for piece in range(PIECES) for _ in range(2)]
    grad_shapes = [jax.ShapeDtypeStruct((count, context, width), BF16) for width in widths]
    aliased = 1 + len(rows) + 4
    return pl.pallas_call(
        functools.partial(attend_kernel, start, count, direct, not carried),
        in_specs=[SMEM] + [VMEM] * len(rows) + [VMEM] * 4 + [HBM] * len(carried),
        out_specs=[HBM] * 2 + [VMEM] * (1 + 2 * PIECES),
        scratch_shapes=[
            pltpu.VMEM((count, tokens, feat), BF16),
            pltpu.VMEM((count, tokens, feat), BF16),
            pltpu.VMEM((count, context, feat), BF16),
            pltpu.VMEM((count, context, feat), BF16),
            pltpu.VMEM((count, context, enc), BF16),
            pltpu.SemaphoreType.DMA((count, 2)),
            pltpu.SMEM((max(direct, 1),), jnp.int32),
        ],
        out_shape=[row_shape, row_shape, turned_shape] + grad_shapes,
        input_output_aliases={aliased: 0, aliased + 1: 1} if carried else {},
        compiler_params=params(ATTEND_MIB),
        name="attend_blocks",
    )(own, *rows, wk, wv, queries, grad_out, *carried)


def weigh_kernel(chunks, carried, last, *refs):
    refs = list(refs)
    take = lambda n: [refs.pop(0) for _ in range(n)]
    turned, grads = take(chunks), [take(chunks) for _ in range(2)]
    before = take(2) if carried else []
    half = turned[0].shape[0] // 2
    dp = lax.axis_index("dp")
    for i in range(2):
        total = before[i][...] if carried else 0.0
        for c in range(chunks):
            grad = grads[i][c][...]
            total += jnp.dot(turned[c][...], grad.reshape(-1, grad.shape[-1]), preferred_element_type=F32)
        if not last:
            refs[i][...] = total
            continue
        refs[-1][...] = total
        for j, side in enumerate((1 - dp, dp)):
            refs[2 * j + i][...] = refs[-1][pl.ds(pl.multiple_of(side * half, half), half), :].astype(BF16)


def weigh(turned, dks, dvs, before, last):
    enc, width = turned[0].shape[0], dks[0].shape[-1]
    shapes = [jax.ShapeDtypeStruct((enc // 2, width), BF16)] * 4 if last else [jax.ShapeDtypeStruct((enc, width), F32)] * 2
    return pl.pallas_call(
        functools.partial(weigh_kernel, len(turned), bool(before), last),
        in_specs=[VMEM] * (3 * len(turned) + len(before)),
        out_specs=[VMEM] * len(shapes),
        out_shape=shapes,
        scratch_shapes=[pltpu.VMEM((enc, width), F32)] if last else [],
        compiler_params=params(WEIGH_MIB),
        name="weigh_grads",
    )(*turned, *dks, *dvs, *before)


def fold_kernel(dims, count, *refs):
    ret = lax.axis_index("ret")
    for i in range(count):
        held_ref, arrived_ref = refs[i], refs[count + i]
        bit, place = dims[i]
        mine = (ret >> bit) & 1
        stride = 1 << place
        for j in range(held_ref.shape[0] // 2):
            base = (j // stride) * 2 * stride + j % stride
            for k, side in enumerate((1 - mine, mine)):
                row = base + side * stride
                total = held_ref[row].astype(F32) + arrived_ref[row].astype(F32)
                refs[(2 + k) * count + i][j] = total.astype(BF16)


def fold(held, arrived, dims):
    count = len(held)
    parts, rows, width = held[0].shape
    shapes = [jax.ShapeDtypeStruct((parts // 2, rows, width), BF16)] * (2 * count)
    return pl.pallas_call(
        functools.partial(fold_kernel, dims, count),
        in_specs=[VMEM] * (2 * count),
        out_specs=[VMEM] * len(shapes),
        out_shape=shapes,
        compiler_params=params(16),
        name="fold_grads",
    )(*held, *arrived)


def join_kernel(*refs):
    count = (len(refs) - 2) // 2
    place = [0, 0]
    for i in range(count):
        total = refs[i][0].astype(F32) + refs[count + i][0].astype(F32)
        width = total.shape[1]
        refs[2 * count + i % 2][:, place[i % 2] : place[i % 2] + width] = total
        place[i % 2] += width


def join(held, arrived):
    rows, feat = held[0].shape[1], sum(part.shape[2] for part in held) // 2
    return pl.pallas_call(
        join_kernel,
        in_specs=[VMEM] * (2 * len(held)),
        out_specs=[VMEM] * 2,
        out_shape=[jax.ShapeDtypeStruct((rows, feat), F32)] * 2,
        compiler_params=params(16),
        name="join_grads",
    )(*held, *arrived)


class Sums:
    def __init__(self, send, held):
        self.bits = lax.axis_size("ret").bit_length() - 1
        self.left = [list(range(self.bits)) for _ in held]
        self.held = self.split(held)
        self.arrived = self.split([swap(grad, "dp", 1) for grad in send])
        self.steps = 0

    def split(self, grads):
        return [grad.reshape(1 << self.bits, -1, grad.shape[-1]) for grad in grads]

    def fold(self):
        self.bit = [self.steps, self.bits - 1 - self.steps]
        dims = tuple((bit, left.index(bit)) for bit, left in zip(self.bit, self.left))
        for bit, left in zip(self.bit, self.left):
            left.remove(bit)
        parts = fold(self.held, self.arrived, dims)
        self.send, self.held = list(parts[:2]), list(parts[2:])
        self.steps += 1

    def exchange(self):
        self.arrived = [swap(grad, "ret", 1 << bit) for grad, bit in zip(self.send, self.bit)]


def spans_of(blocks):
    spans, start = [], 0
    for count, pair in CHUNKS:
        spans.append((start, count, pair))
        start += count
    return spans if start == blocks else [(0, blocks, False)]


def local(queries, enc_states, w_key, w_value, shard_ids, row_ids, grad_out):
    n_ret = lax.axis_size("ret")
    blocks = shard_ids.shape[1]
    bound = blocks * NEIGHBOURS * 2 // n_ret
    enc = enc_states.shape[2]

    def capacity(count):
        return min(count, bound)

    own = jnp.stack([shard_ids[0], row_ids[0]], axis=-1).reshape(-1)
    ids = exchange_ids(own)
    normed = normalize_rows(enc_states[0]).reshape(-1, 2, HALF, enc)
    spans = spans_of(blocks)
    outgoing = pick(ids, normed, spans[:1], capacity)
    if len(spans) > 1:
        outgoing = outgoing + pick(ids, normed, spans[1:], capacity)
    query_blocks, grad_blocks = (array.reshape(blocks, -1, array.shape[2]) for array in (queries, grad_out))
    carried, arrivals = [], []
    for slots in outgoing:
        slots = list(slots)
        if arrivals:
            for k in range(1, n_ret):
                arrivals[-1][k], slots[k] = lax.optimization_barrier((arrivals[-1][k], slots[k]))
        arrivals.append(slots[:1] + [swap(slots[k], "ret", k) for k in range(1, n_ret)])
    rows, turned, found, sums, early = [None] * len(spans), [], [], [[]] * PIECES, None

    def weigh_piece(turned, found, piece, before, last):
        return list(weigh(turned, *([grads[2 * piece + i] for grads in found] for i in range(2)), before, last))


    def prepare(i):
        start, count, pair = spans[i]
        if pair:
            mine = unpack(own, arrivals[i], start, count)
            rows[i] = [mine, swap(mine, "ctx", 1)]
        else:
            rows[i] = arrivals[i]

    prepare(0)
    for i, (start, count, pair) in enumerate(spans):
        last = i + 1 == len(spans)
        if not last and spans[i + 1][2]:
            prepare(i + 1)
            rows[i][0], rows[i + 1][0] = lax.optimization_barrier((rows[i][0], rows[i + 1][0]))
        attended, grad_queries, flipped, *grads = attend(rows[i], own, w_key, w_value, query_blocks, grad_blocks, start, count, carried)
        carried = [attended, grad_queries]
        turned.append(flipped)
        found.append(grads)
        if i == 0 and not last:
            early = turned, found
            turned, found = [], []
            sums[0] = weigh_piece(*early, 0, [], False)
            sums[0][0], rows[1][0] = lax.optimization_barrier((sums[0][0], rows[1][0]))
        if not last and rows[i + 1] is None:
            carried[0], arrivals[i + 1] = lax.optimization_barrier((carried[0], arrivals[i + 1]))
            prepare(i + 1)
    states, parts = [], None
    for piece in range(PIECES):
        if parts:
            if early:
                parts[0], early[0][0] = lax.optimization_barrier((parts[0], early[0][0]))
                sums[piece] = weigh_piece(*early, piece, [], False)
            states.append(Sums(parts[:2], parts[2:]))
            states[-1].fold()
            states[-1].send, turned[0] = lax.optimization_barrier((states[-1].send, turned[0]))
        parts = weigh_piece(turned, found, piece, sums[piece], True)
    states.append(Sums(parts[:2], parts[2:]))
    states[-1].fold()
    for step in range(states[0].bits):
        for state in states:
            if step:
                state.fold()
            state.exchange()
    attended, grad_queries = carried
    grad_w_key, grad_w_value = join(sum([state.held for state in states], []), sum([state.arrived for state in states], []))
    return attended.reshape(queries.shape), grad_queries.reshape(queries.shape), grad_w_key, grad_w_value


def solution(mesh):
    placed = (
        P("dp", "ret", "ctx"),
        P("dp", "ret", None),
        P(None, "ctx"),
        P(None, "ctx"),
        P("dp", "ret", None),
        P("dp", "ret", None),
        P("dp", "ret", "ctx"),
    )
    return jax.shard_map(
        local,
        mesh=mesh,
        in_specs=placed,
        out_specs=(
            P("dp", "ret", "ctx"),
            P("dp", "ret", "ctx"),
            P(("dp", "ret"), "ctx"),
            P(("dp", "ret"), "ctx"),
        ),
        check_vma=False,
    )
```

```python
import functools
import math

import jax
import jax.numpy as jnp
from jax import lax
from jax.experimental import pallas as pl
from jax.experimental.pallas import tpu as pltpu
from jax.sharding import PartitionSpec as P

HEAD_DIM = 128
NEIGH_LEN = 128
NEIGHBOURS = 2
HALF = NEIGH_LEN // 2
MIB = 1024 * 1024
ATTEND_MIB = 26
WEIGH_MIB = 26
PIECES = 2
PROJECT_FIRST = True
MERGE = False
FIRST_PIECE = 6 / 8
CHUNKS = ((3, True), (3, True), (2, False))

F32 = jnp.float32
BF16 = jnp.bfloat16
ANY = pl.BlockSpec(memory_space=pl.ANY)
SMEM = pl.BlockSpec(memory_space=pltpu.SMEM)
VMEM = pl.BlockSpec(memory_space=pltpu.VMEM)
HBM = pl.BlockSpec(memory_space=pltpu.HBM)


def params(mib):
    return pltpu.CompilerParams(vmem_limit_bytes=mib * MIB)


def piece_heads(heads):
    return [0, int(heads * FIRST_PIECE), heads]


def contract(lhs, rhs, dims):
    return lax.dot_general(lhs, rhs, (dims, ((), ())), preferred_element_type=F32)


def swap(array, axis, bit):
    size = lax.axis_size(axis)
    return lax.ppermute(array, axis, [(i, i ^ bit) for i in range(size)])


def normalize_kernel(states_ref, out_ref):
    floats = states_ref[...].astype(F32)
    mean_square = jnp.mean(floats * floats, axis=-1, keepdims=True)
    out_ref[...] = (floats * lax.rsqrt(mean_square + 1e-06)).astype(BF16)


def normalize_rows(states):
    rows, width = states.shape
    tile = 512
    spec = pl.BlockSpec((tile, width), lambda i: (i, 0))
    return pl.pallas_call(
        normalize_kernel,
        grid=(rows // tile,),
        in_specs=[spec],
        out_specs=spec,
        out_shape=jax.ShapeDtypeStruct(states.shape, BF16),
        compiler_params=params(12),
        name="normalize_rows",
    )(states)


def exchange_ids(own):
    n_ret = lax.axis_size("ret")
    if n_ret <= 4:
        return jnp.stack([own] + [swap(own, "ret", k) for k in range(1, n_ret)])
    every = lax.all_gather(own, "ret")
    order = jnp.arange(n_ret, dtype=jnp.int32) ^ lax.axis_index("ret")
    return jnp.take(every, order, axis=0)


def pick_kernel(spans, id_ref, normed_ref, *outs):
    n_ret = id_ref.shape[0]
    me = lax.axis_index("ret")
    part = lax.rem(lax.axis_index("ctx"), 2)
    for chunk, (start, count, pair) in enumerate(spans):
        for k in range(n_ret):
            out_ref = outs[chunk * n_ret + k]

            def send(i, used, k=k, start=start, pair=pair, out_ref=out_ref):
                request = (start * NEIGHBOURS + i) * 2
                mine = id_ref[k, request] == me

                @pl.when(mine)
                def _():
                    row = id_ref[k, request + 1]
                    out_ref[used] = normed_ref[row, part] if pair else normed_ref[row]

                return used + jnp.where(mine, 1, 0)

            lax.fori_loop(0, count * NEIGHBOURS, send, jnp.int32(0))


def pick(ids, normed, spans, capacity):
    n_ret, width = ids.shape[0], normed.shape[-1]
    slots = [capacity(count) for _, count, _ in spans]
    shapes = [(cap, HALF, width) if pair else (cap, 2, HALF, width) for (_, _, pair), cap in zip(spans, slots)]
    shapes = [jax.ShapeDtypeStruct(shape, BF16) for shape in shapes for _ in range(n_ret)]
    picked = pl.pallas_call(
        functools.partial(pick_kernel, spans),
        in_specs=[SMEM, VMEM],
        out_specs=[VMEM] * len(shapes),
        out_shape=shapes,
        compiler_params=params(16),
        name="pick_rows",
    )(ids, normed)
    return [picked[i : i + n_ret] for i in range(0, len(picked), n_ret)]


def unpack_kernel(start, count, id_ref, *refs):
    *incoming, out_ref, ranks = refs
    place_rows(start, count, id_ref, incoming, ranks, lambda i: out_ref.at[i])


def place_rows(start, count, id_ref, incoming, ranks, target):
    me = lax.axis_index("ret")
    for k in range(len(incoming)):
        ranks[k] = 0
    for i in range(count * NEIGHBOURS):
        source = id_ref[(start * NEIGHBOURS + i) * 2] ^ me
        rank = ranks[source]
        ranks[source] = rank + 1
        for k in range(len(incoming)):

            @pl.when(source == k)
            def _(k=k, rank=rank, i=i):
                target(i)[...] = incoming[k][rank]


def unpack(own, incoming, start, count):
    return pl.pallas_call(
        functools.partial(unpack_kernel, start, count),
        in_specs=[SMEM] + [VMEM] * len(incoming),
        out_specs=VMEM,
        out_shape=jax.ShapeDtypeStruct((count * NEIGHBOURS,) + incoming[0].shape[1:], BF16),
        scratch_shapes=[pltpu.SMEM((len(incoming),), jnp.int32)],
        compiler_params=params(8),
        name="unpack_rows",
    )(own, *incoming)


def block_grads(keys, values, query, grad, out_ref, gq_ref, grad_refs):
    scale = 1.0 / math.sqrt(HEAD_DIM)
    tokens, heads = out_ref.shape[0], out_ref.shape[1] // HEAD_DIM
    zero = jnp.zeros((tokens, HEAD_DIM), BF16)
    bounds = piece_heads(heads)
    cols = [slice(head * HEAD_DIM, (head + 1) * HEAD_DIM) for head in range(heads)]

    def reader(head):
        upper = jnp.concatenate([query(cols[head]), zero], axis=1)
        lower = jnp.concatenate([zero, grad(cols[head])], axis=1)
        return jnp.concatenate([upper, lower], axis=0)

    def both(head):
        return jnp.concatenate([keys(cols[head]), values(cols[head])], axis=1)

    def finish(head, probs, dscore):
        mixed = jnp.dot(jnp.concatenate([probs, dscore], axis=0), both(head), preferred_element_type=F32)
        out_ref[:, cols[head]] = mixed[:tokens, HEAD_DIM:].astype(BF16)
        gq_ref[:, cols[head]] = mixed[tokens:, :HEAD_DIM].astype(BF16)
        grads = contract(jnp.concatenate([dscore, probs], axis=0), reader(head), ((0,), (0,))).astype(BF16)
        piece = int(head >= bounds[1])
        place = cols[head - bounds[piece]]
        grad_refs[2 * piece][:, place] = grads[:, :HEAD_DIM]
        grad_refs[2 * piece + 1][:, place] = grads[:, HEAD_DIM:]

    ahead, lag = 3, 2
    products, weights = {}, {}
    for head in range(-ahead, heads + lag):
        if 0 <= head + ahead < heads:
            products[head + ahead] = contract(reader(head + ahead), both(head + ahead), ((1,), (1,)))
        if 0 <= head < heads:
            product = products.pop(head)
            expo, dprob = jnp.exp(product[:tokens] * scale), product[tokens:]
            inverse = 1.0 / jnp.sum(expo, axis=-1, keepdims=True)
            delta = jnp.sum(expo * dprob, axis=-1, keepdims=True) * inverse
            probs = expo * inverse
            weights[head] = (probs.astype(BF16), (probs * (dprob - delta) * scale).astype(BF16))
        if 0 <= head - lag < heads:
            finish(head - lag, *weights.pop(head - lag))


def project_kernel(rows_ref, wk_ref, wv_ref, k_ref, v_ref):
    rows = rows_ref[...].reshape(-1, rows_ref.shape[-1])
    for w_ref, target in ((wk_ref, k_ref), (wv_ref, v_ref)):
        target[...] = jnp.dot(rows, w_ref[...], preferred_element_type=F32).astype(BF16).reshape(target.shape)


def project(rows, wk, wv):
    count, feat = rows.shape[0] // NEIGHBOURS, wk.shape[1]
    shape = jax.ShapeDtypeStruct((count, NEIGHBOURS * rows.shape[1], feat), BF16)
    return pl.pallas_call(
        project_kernel,
        in_specs=[VMEM] * 3,
        out_specs=[VMEM] * 2,
        out_shape=[shape] * 2,
        compiler_params=params(16),
        name="project_rows",
    )(rows, wk, wv)


def weigh_sum(turned, grads, before):
    total = 0.0 if before is None else before[...]
    for turn, grad in zip(turned, grads):
        values = grad[...]
        total += jnp.dot(turn[...], values.reshape(-1, values.shape[-1]), preferred_element_type=F32)
    return total


def weigh_halves(total, scratch, targets):
    half = scratch.shape[0] // 2
    dp = lax.axis_index("dp")
    scratch[...] = total
    for target, side in zip(targets, (1 - dp, dp)):
        target[...] = scratch[pl.ds(pl.multiple_of(side * half, half), half), :].astype(BF16)


def attend_kernel(start, count, sources, pair, done, first, tail, id_ref, *refs):
    refs = list(refs)
    take = lambda n: [refs.pop(0) for _ in range(n)]
    row_refs = take(sources)
    ready = take(2 if done else 0)
    wk_ref, wv_ref, q_ref, go_ref = take(4)
    tail_refs = take(3 * tail + 2 if tail else 0)
    take(0 if first else 2)
    out_hbm, gq_hbm, turned = take(3)
    grad_refs = take(2 * PIECES)
    tail_outs = take(4 if tail else 0)
    out_ref, gq_ref, keys, values, rows, sems, ranks = take(7)
    size, width = rows.shape[1:]
    part, feat = keys.shape[1:]
    if pair:
        for i, ref in enumerate(row_refs):
            rows[:, i * (size // 2) : (i + 1) * (size // 2)] = ref[...].reshape(count, size // 2, width)
    else:
        place_rows(start, count, id_ref, row_refs, ranks, lambda i: rows.at[i // NEIGHBOURS, pl.ds(i % NEIGHBOURS * NEIGH_LEN, NEIGH_LEN)])

    rest = (row_refs[1] if done else rows)[...].reshape(-1, width)
    for w_ref, target in ((wk_ref, keys), (wv_ref, values)):
        product = jnp.dot(rest, w_ref[...], preferred_element_type=F32).astype(BF16)
        target[...] = product.reshape(count, part, feat)

    def stores(b):
        pairs = ((out_ref, out_hbm), (gq_ref, gq_hbm))
        return [pltpu.make_async_copy(src.at[b], dst.at[start + b], sems.at[b, i]) for i, (src, dst) in enumerate(pairs)]

    def block(b, carry):
        def pick(at, *parts):
            return lambda cols: jnp.concatenate([ref[at, :, cols] for ref in parts], axis=0)

        context = pick(b, *ready[:1], keys), pick(b, *ready[1:], values)
        block_grads(*context, pick(start + b, q_ref), pick(start + b, go_ref), out_ref.at[b], gq_ref.at[b], [ref.at[b] for ref in grad_refs])
        for store in stores(b):
            store.start()
        return carry

    lax.fori_loop(0, count, block, 0)
    turned[...] = rows[...].reshape(-1, width).T
    if tail:
        for i in range(2):
            total = weigh_sum(tail_refs[:tail] + [turned], tail_refs[(1 + i) * tail : (2 + i) * tail] + [grad_refs[i]], tail_refs[3 * tail + i])
            weigh_halves(total, refs[0], tail_outs[i::2])
    for b in range(count):
        for store in stores(b):
            store.wait()


def attend(rows, ready, own, wk, wv, queries, grad_out, start, count, pair, carried, tail):
    _, tokens, feat = queries.shape
    enc = wk.shape[0]
    context = NEIGHBOURS * NEIGH_LEN
    row_shape = jax.ShapeDtypeStruct(queries.shape, BF16)
    if not pair:
        rows = [part.reshape(part.shape[0], NEIGH_LEN, enc) for part in rows]
    turned_shape = jax.ShapeDtypeStruct((enc, count * context), BF16)
    bounds = piece_heads(feat // HEAD_DIM)
    widths = [(bounds[piece + 1] - bounds[piece]) * HEAD_DIM for piece in range(PIECES) for _ in range(2)]
    grad_shapes = [jax.ShapeDtypeStruct((count, context, width), BF16) for width in widths]
    fresh = context // 2 if ready else context
    weighed = [jax.ShapeDtypeStruct((enc // 2, widths[0]), BF16)] * (4 if tail else 0)
    aliased = 1 + len(rows) + len(ready) + 4 + len(tail)
    settings = start, count, len(rows), pair, bool(ready), not carried, len(tail) // 3
    return pl.pallas_call(
        functools.partial(attend_kernel, *settings),
        in_specs=[SMEM] + [VMEM] * (len(rows) + len(ready) + 4 + len(tail)) + [HBM] * len(carried),
        out_specs=[HBM] * 2 + [VMEM] * (1 + 2 * PIECES + len(weighed)),
        scratch_shapes=[
            pltpu.VMEM((count, tokens, feat), BF16),
            pltpu.VMEM((count, tokens, feat), BF16),
            pltpu.VMEM((count, fresh, feat), BF16),
            pltpu.VMEM((count, fresh, feat), BF16),
            pltpu.VMEM((count, context, enc), BF16),
            pltpu.SemaphoreType.DMA((count, 2)),
            pltpu.SMEM((len(rows),), jnp.int32),
        ]
        + [pltpu.VMEM((enc, widths[0]), F32)] * bool(tail),
        out_shape=[row_shape, row_shape, turned_shape] + grad_shapes + weighed,
        input_output_aliases={aliased: 0, aliased + 1: 1} if carried else {},
        compiler_params=params(ATTEND_MIB),
        name="attend_blocks",
    )(own, *rows, *ready, wk, wv, queries, grad_out, *tail, *carried)


def weigh_kernel(chunks, carried, last, *refs):
    refs = list(refs)
    take = lambda n: [refs.pop(0) for _ in range(n)]
    turned, grads = take(chunks), [take(chunks) for _ in range(2)]
    before = take(2) if carried else [None] * 2
    for i in range(2):
        total = weigh_sum(turned, grads[i], before[i])
        if last:
            weigh_halves(total, refs[-1], refs[i:4:2])
        else:
            refs[i][...] = total


def weigh(turned, dks, dvs, before, last):
    enc, width = turned[0].shape[0], dks[0].shape[-1]
    shapes = [jax.ShapeDtypeStruct((enc // 2, width), BF16)] * 4 if last else [jax.ShapeDtypeStruct((enc, width), F32)] * 2
    return pl.pallas_call(
        functools.partial(weigh_kernel, len(turned), bool(before), last),
        in_specs=[VMEM] * (3 * len(turned) + len(before)),
        out_specs=[VMEM] * len(shapes),
        out_shape=shapes,
        scratch_shapes=[pltpu.VMEM((enc, width), F32)] if last else [],
        compiler_params=params(WEIGH_MIB),
        name="weigh_grads",
    )(*turned, *dks, *dvs, *before)


def fold_kernel(dims, count, *refs):
    ret = lax.axis_index("ret")
    for i in range(count):
        held_ref, arrived_ref = refs[i], refs[count + i]
        bit, place = dims[i]
        mine = (ret >> bit) & 1
        stride = 1 << place
        for j in range(held_ref.shape[0] // 2):
            base = (j // stride) * 2 * stride + j % stride
            for k, side in enumerate((1 - mine, mine)):
                row = base + side * stride
                total = held_ref[row].astype(F32) + arrived_ref[row].astype(F32)
                refs[(2 + k) * count + i][j] = total.astype(BF16)


def fold(held, arrived, dims):
    count = len(held)
    parts, rows, width = held[0].shape
    shapes = [jax.ShapeDtypeStruct((parts // 2, rows, width), BF16)] * (2 * count)
    return pl.pallas_call(
        functools.partial(fold_kernel, dims, count),
        in_specs=[VMEM] * (2 * count),
        out_specs=[VMEM] * len(shapes),
        out_shape=shapes,
        compiler_params=params(16),
        name="fold_grads",
    )(*held, *arrived)


def join_kernel(*refs):
    count = (len(refs) - 2) // 2
    place = [0, 0]
    for i in range(count):
        total = refs[i][0].astype(F32) + refs[count + i][0].astype(F32)
        width = total.shape[1]
        refs[2 * count + i % 2][:, place[i % 2] : place[i % 2] + width] = total
        place[i % 2] += width


def join(held, arrived):
    rows, feat = held[0].shape[1], sum(part.shape[2] for part in held) // 2
    return pl.pallas_call(
        join_kernel,
        in_specs=[VMEM] * (2 * len(held)),
        out_specs=[VMEM] * 2,
        out_shape=[jax.ShapeDtypeStruct((rows, feat), F32)] * 2,
        compiler_params=params(16),
        name="join_grads",
    )(*held, *arrived)


class Sums:
    def __init__(self, send, held):
        self.bits = lax.axis_size("ret").bit_length() - 1
        self.left = [list(range(self.bits)) for _ in held]
        self.held = self.split(held)
        self.arrived = self.split([swap(grad, "dp", 1) for grad in send])
        self.steps = 0

    def split(self, grads):
        return [grad.reshape(1 << self.bits, -1, grad.shape[-1]) for grad in grads]

    def fold(self):
        self.bit = [self.steps, self.bits - 1 - self.steps]
        dims = tuple((bit, left.index(bit)) for bit, left in zip(self.bit, self.left))
        for bit, left in zip(self.bit, self.left):
            left.remove(bit)
        parts = fold(self.held, self.arrived, dims)
        self.send, self.held = list(parts[:2]), list(parts[2:])
        self.steps += 1

    def exchange(self):
        self.arrived = [swap(grad, "ret", 1 << bit) for grad, bit in zip(self.send, self.bit)]


def spans_of(blocks):
    spans, start = [], 0
    for count, pair in CHUNKS:
        spans.append((start, count, pair))
        start += count
    return spans if start == blocks else [(0, blocks, False)]


def local(queries, enc_states, w_key, w_value, shard_ids, row_ids, grad_out):
    n_ret = lax.axis_size("ret")
    blocks = shard_ids.shape[1]
    bound = blocks * NEIGHBOURS * 2 // n_ret
    enc = enc_states.shape[2]

    def capacity(count):
        return min(count, bound)

    own = jnp.stack([shard_ids[0], row_ids[0]], axis=-1).reshape(-1)
    ids = exchange_ids(own)
    normed = normalize_rows(enc_states[0]).reshape(-1, 2, HALF, enc)
    spans = spans_of(blocks)
    outgoing = pick(ids, normed, spans[:1], capacity)
    if len(spans) > 1:
        outgoing = outgoing + pick(ids, normed, spans[1:], capacity)
    query_blocks, grad_blocks = (array.reshape(blocks, -1, array.shape[2]) for array in (queries, grad_out))
    carried, arrivals = [], []
    for slots in outgoing:
        slots = list(slots)
        if arrivals:
            for k in range(1, n_ret):
                arrivals[-1][k], slots[k] = lax.optimization_barrier((arrivals[-1][k], slots[k]))
        arrivals.append(slots[:1] + [swap(slots[k], "ret", k) for k in range(1, n_ret)])
    rows, turned, found, sums, early = [None] * len(spans), [], [], [[]] * PIECES, None
    ready = [[] for _ in spans]

    def weigh_piece(turned, found, piece, before, last):
        return list(weigh(turned, *([grads[2 * piece + i] for grads in found] for i in range(2)), before, last))


    def prepare(i):
        start, count, pair = spans[i]
        if pair:
            mine = unpack(own, arrivals[i], start, count)
            rows[i] = [mine, swap(mine, "ctx", 1)]
            if PROJECT_FIRST:
                ready[i] = list(project(mine, w_key, w_value))
        else:
            rows[i] = arrivals[i]

    prepare(0)
    for i, (start, count, pair) in enumerate(spans):
        last = i + 1 == len(spans)
        if not last and spans[i + 1][2]:
            if ready[i]:
                ready[i][0], arrivals[i + 1] = lax.optimization_barrier((ready[i][0], arrivals[i + 1]))
            prepare(i + 1)
            rows[i][0], rows[i + 1][0] = lax.optimization_barrier((rows[i][0], rows[i + 1][0]))
        tail = []
        if MERGE and last and early and found:
            tail = turned + [grads[n] for n in range(2) for grads in found] + sums[0]
        results = attend(rows[i], ready[i], own, w_key, w_value, query_blocks, grad_blocks, start, count, pair, carried, tail)
        attended, grad_queries, flipped = results[:3]
        grads, parts = results[3 : 3 + 2 * PIECES], list(results[3 + 2 * PIECES :])
        carried = [attended, grad_queries]
        turned.append(flipped)
        found.append(grads)
        if i == 0 and not last:
            early = turned, found
            turned, found = [], []
            sums[0] = weigh_piece(*early, 0, [], False)
            sums[0][0], rows[1][0] = lax.optimization_barrier((sums[0][0], rows[1][0]))
        if not last and rows[i + 1] is None:
            carried[0], arrivals[i + 1] = lax.optimization_barrier((carried[0], arrivals[i + 1]))
            prepare(i + 1)
    states = []
    for piece in range(PIECES):
        if piece:
            if early:
                parts[0], early[0][0] = lax.optimization_barrier((parts[0], early[0][0]))
                sums[piece] = weigh_piece(*early, piece, [], False)
            states.append(Sums(parts[:2], parts[2:]))
            states[-1].fold()
            states[-1].send, turned[0] = lax.optimization_barrier((states[-1].send, turned[0]))
        if piece or not parts:
            parts = weigh_piece(turned, found, piece, sums[piece], True)
    states.append(Sums(parts[:2], parts[2:]))
    states[-1].fold()
    for step in range(states[0].bits):
        for state in states:
            if step:
                state.fold()
            state.exchange()
    attended, grad_queries = carried
    grad_w_key, grad_w_value = join(sum([state.held for state in states], []), sum([state.arrived for state in states], []))
    return attended.reshape(queries.shape), grad_queries.reshape(queries.shape), grad_w_key, grad_w_value


def solution(mesh):
    placed = (
        P("dp", "ret", "ctx"),
        P("dp", "ret", None),
        P(None, "ctx"),
        P(None, "ctx"),
        P("dp", "ret", None),
        P("dp", "ret", None),
        P("dp", "ret", "ctx"),
    )
    return jax.shard_map(
        local,
        mesh=mesh,
        in_specs=placed,
        out_specs=(
            P("dp", "ret", "ctx"),
            P("dp", "ret", "ctx"),
            P(("dp", "ret"), "ctx"),
            P(("dp", "ret"), "ctx"),
        ),
        check_vma=False,
    )
```

```python
import functools
import math

import jax
import jax.numpy as jnp
from jax import lax
from jax.experimental import pallas as pl
from jax.experimental.pallas import tpu as pltpu
from jax.sharding import PartitionSpec as P

HEAD_DIM = 128
NEIGH_LEN = 128
NEIGHBOURS = 2
HALF = NEIGH_LEN // 2
MIB = 1024 * 1024
ATTEND_MIB = 26
WEIGH_MIB = 26
PIECES = 2
SIDES = (((False,), (True,)), ((False, True),))
PROJECT_FIRST = True
FIRST_PIECE = 6 / 8
CHUNKS = ((3, True), (3, True), (2, False))

F32 = jnp.float32
BF16 = jnp.bfloat16
ANY = pl.BlockSpec(memory_space=pl.ANY)
SMEM = pl.BlockSpec(memory_space=pltpu.SMEM)
VMEM = pl.BlockSpec(memory_space=pltpu.VMEM)
HBM = pl.BlockSpec(memory_space=pltpu.HBM)


def params(mib):
    return pltpu.CompilerParams(vmem_limit_bytes=mib * MIB)


def piece_heads(heads):
    return [0, int(heads * FIRST_PIECE), heads]


def contract(lhs, rhs, dims):
    return lax.dot_general(lhs, rhs, (dims, ((), ())), preferred_element_type=F32)


def swap(array, axis, bit):
    size = lax.axis_size(axis)
    return lax.ppermute(array, axis, [(i, i ^ bit) for i in range(size)])


def normalize_kernel(states_ref, out_ref):
    floats = states_ref[...].astype(F32)
    mean_square = jnp.mean(floats * floats, axis=-1, keepdims=True)
    out_ref[...] = (floats * lax.rsqrt(mean_square + 1e-06)).astype(BF16)


def normalize_rows(states):
    rows, width = states.shape
    tile = 512
    spec = pl.BlockSpec((tile, width), lambda i: (i, 0))
    return pl.pallas_call(
        normalize_kernel,
        grid=(rows // tile,),
        in_specs=[spec],
        out_specs=spec,
        out_shape=jax.ShapeDtypeStruct(states.shape, BF16),
        compiler_params=params(12),
        name="normalize_rows",
    )(states)


def exchange_ids(own):
    n_ret = lax.axis_size("ret")
    if n_ret <= 4:
        return jnp.stack([own] + [swap(own, "ret", k) for k in range(1, n_ret)])
    every = lax.all_gather(own, "ret")
    order = jnp.arange(n_ret, dtype=jnp.int32) ^ lax.axis_index("ret")
    return jnp.take(every, order, axis=0)


def pick_kernel(spans, id_ref, normed_ref, *outs):
    n_ret = id_ref.shape[0]
    me = lax.axis_index("ret")
    part = lax.rem(lax.axis_index("ctx"), 2)
    for chunk, (start, count, pair) in enumerate(spans):
        for k in range(n_ret):
            out_ref = outs[chunk * n_ret + k]

            def send(i, used, k=k, start=start, pair=pair, out_ref=out_ref):
                request = (start * NEIGHBOURS + i) * 2
                mine = id_ref[k, request] == me

                @pl.when(mine)
                def _():
                    row = id_ref[k, request + 1]
                    out_ref[used] = normed_ref[row, part] if pair else normed_ref[row]

                return used + jnp.where(mine, 1, 0)

            lax.fori_loop(0, count * NEIGHBOURS, send, jnp.int32(0))


def pick(ids, normed, spans, capacity):
    n_ret, width = ids.shape[0], normed.shape[-1]
    slots = [capacity(count) for _, count, _ in spans]
    shapes = [(cap, HALF, width) if pair else (cap, 2, HALF, width) for (_, _, pair), cap in zip(spans, slots)]
    shapes = [jax.ShapeDtypeStruct(shape, BF16) for shape in shapes for _ in range(n_ret)]
    picked = pl.pallas_call(
        functools.partial(pick_kernel, spans),
        in_specs=[SMEM, VMEM],
        out_specs=[VMEM] * len(shapes),
        out_shape=shapes,
        compiler_params=params(16),
        name="pick_rows",
    )(ids, normed)
    return [picked[i : i + n_ret] for i in range(0, len(picked), n_ret)]


def unpack_kernel(start, count, id_ref, *refs):
    *incoming, out_ref, ranks = refs
    place_rows(start, count, id_ref, incoming, ranks, lambda i: out_ref.at[i])


def place_rows(start, count, id_ref, incoming, ranks, target):
    me = lax.axis_index("ret")
    for k in range(len(incoming)):
        ranks[k] = 0
    for i in range(count * NEIGHBOURS):
        source = id_ref[(start * NEIGHBOURS + i) * 2] ^ me
        rank = ranks[source]
        ranks[source] = rank + 1
        for k in range(len(incoming)):

            @pl.when(source == k)
            def _(k=k, rank=rank, i=i):
                target(i)[...] = incoming[k][rank]


def unpack(own, incoming, start, count):
    return pl.pallas_call(
        functools.partial(unpack_kernel, start, count),
        in_specs=[SMEM] + [VMEM] * len(incoming),
        out_specs=VMEM,
        out_shape=jax.ShapeDtypeStruct((count * NEIGHBOURS,) + incoming[0].shape[1:], BF16),
        scratch_shapes=[pltpu.SMEM((len(incoming),), jnp.int32)],
        compiler_params=params(8),
        name="unpack_rows",
    )(own, *incoming)


def block_grads(keys, values, query, grad, out_ref, gq_ref, grad_refs):
    scale = 1.0 / math.sqrt(HEAD_DIM)
    tokens, heads = out_ref.shape[0], out_ref.shape[1] // HEAD_DIM
    zero = jnp.zeros((tokens, HEAD_DIM), BF16)
    bounds = piece_heads(heads)
    cols = [slice(head * HEAD_DIM, (head + 1) * HEAD_DIM) for head in range(heads)]

    def reader(head):
        upper = jnp.concatenate([query(cols[head]), zero], axis=1)
        lower = jnp.concatenate([zero, grad(cols[head])], axis=1)
        return jnp.concatenate([upper, lower], axis=0)

    def both(head):
        return jnp.concatenate([keys(cols[head]), values(cols[head])], axis=1)

    def finish(head, probs, dscore):
        mixed = jnp.dot(jnp.concatenate([probs, dscore], axis=0), both(head), preferred_element_type=F32)
        out_ref[:, cols[head]] = mixed[:tokens, HEAD_DIM:].astype(BF16)
        gq_ref[:, cols[head]] = mixed[tokens:, :HEAD_DIM].astype(BF16)
        grads = contract(jnp.concatenate([dscore, probs], axis=0), reader(head), ((0,), (0,))).astype(BF16)
        piece = int(head >= bounds[1])
        place = cols[head - bounds[piece]]
        grad_refs[2 * piece][:, place] = grads[:, :HEAD_DIM]
        grad_refs[2 * piece + 1][:, place] = grads[:, HEAD_DIM:]

    ahead, lag = 3, 2
    products, weights = {}, {}
    for head in range(-ahead, heads + lag):
        if 0 <= head + ahead < heads:
            products[head + ahead] = contract(reader(head + ahead), both(head + ahead), ((1,), (1,)))
        if 0 <= head < heads:
            product = products.pop(head)
            expo, dprob = jnp.exp(product[:tokens] * scale), product[tokens:]
            inverse = 1.0 / jnp.sum(expo, axis=-1, keepdims=True)
            delta = jnp.sum(expo * dprob, axis=-1, keepdims=True) * inverse
            probs = expo * inverse
            weights[head] = (probs.astype(BF16), (probs * (dprob - delta) * scale).astype(BF16))
        if 0 <= head - lag < heads:
            finish(head - lag, *weights.pop(head - lag))


def project_kernel(rows_ref, wk_ref, wv_ref, k_ref, v_ref):
    rows = rows_ref[...].reshape(-1, rows_ref.shape[-1])
    for w_ref, target in ((wk_ref, k_ref), (wv_ref, v_ref)):
        target[...] = jnp.dot(rows, w_ref[...], preferred_element_type=F32).astype(BF16).reshape(target.shape)


def project(rows, wk, wv):
    count, feat = rows.shape[0] // NEIGHBOURS, wk.shape[1]
    shape = jax.ShapeDtypeStruct((count, NEIGHBOURS * rows.shape[1], feat), BF16)
    return pl.pallas_call(
        project_kernel,
        in_specs=[VMEM] * 3,
        out_specs=[VMEM] * 2,
        out_shape=[shape] * 2,
        compiler_params=params(16),
        name="project_rows",
    )(rows, wk, wv)


def attend_kernel(start, count, sources, pair, done, first, id_ref, *refs):
    refs = list(refs)
    take = lambda n: [refs.pop(0) for _ in range(n)]
    row_refs = take(sources)
    ready = take(2 if done else 0)
    wk_ref, wv_ref, q_ref, go_ref = take(4)
    take(0 if first else 2)
    out_hbm, gq_hbm, turned = take(3)
    grad_refs = take(2 * PIECES)
    out_ref, gq_ref, keys, values, rows, sems, ranks = take(7)
    size, width = rows.shape[1:]
    part, feat = keys.shape[1:]
    if pair:
        for i, ref in enumerate(row_refs):
            rows[:, i * (size // 2) : (i + 1) * (size // 2)] = ref[...].reshape(count, size // 2, width)
    else:
        place_rows(start, count, id_ref, row_refs, ranks, lambda i: rows.at[i // NEIGHBOURS, pl.ds(i % NEIGHBOURS * NEIGH_LEN, NEIGH_LEN)])

    rest = (row_refs[1] if done else rows)[...].reshape(-1, width)
    for w_ref, target in ((wk_ref, keys), (wv_ref, values)):
        product = jnp.dot(rest, w_ref[...], preferred_element_type=F32).astype(BF16)
        target[...] = product.reshape(count, part, feat)

    def stores(b):
        pairs = ((out_ref, out_hbm), (gq_ref, gq_hbm))
        return [pltpu.make_async_copy(src.at[b], dst.at[start + b], sems.at[b, i]) for i, (src, dst) in enumerate(pairs)]

    def block(b, carry):
        def pick(at, *parts):
            return lambda cols: jnp.concatenate([ref[at, :, cols] for ref in parts], axis=0)

        context = pick(b, *ready[:1], keys), pick(b, *ready[1:], values)
        block_grads(*context, pick(start + b, q_ref), pick(start + b, go_ref), out_ref.at[b], gq_ref.at[b], [ref.at[b] for ref in grad_refs])
        for store in stores(b):
            store.start()
        return carry

    lax.fori_loop(0, count, block, 0)
    turned[...] = rows[...].reshape(-1, width).T
    for b in range(count):
        for store in stores(b):
            store.wait()


def attend(rows, ready, own, wk, wv, queries, grad_out, start, count, pair, carried):
    _, tokens, feat = queries.shape
    enc = wk.shape[0]
    context = NEIGHBOURS * NEIGH_LEN
    row_shape = jax.ShapeDtypeStruct(queries.shape, BF16)
    if not pair:
        rows = [part.reshape(part.shape[0], NEIGH_LEN, enc) for part in rows]
    turned_shape = jax.ShapeDtypeStruct((enc, count * context), BF16)
    bounds = piece_heads(feat // HEAD_DIM)
    widths = [(bounds[piece + 1] - bounds[piece]) * HEAD_DIM for piece in range(PIECES) for _ in range(2)]
    grad_shapes = [jax.ShapeDtypeStruct((count, context, width), BF16) for width in widths]
    fresh = context // 2 if ready else context
    aliased = 1 + len(rows) + len(ready) + 4
    settings = start, count, len(rows), pair, bool(ready), not carried
    return pl.pallas_call(
        functools.partial(attend_kernel, *settings),
        in_specs=[SMEM] + [VMEM] * (len(rows) + len(ready) + 4) + [HBM] * len(carried),
        out_specs=[HBM] * 2 + [VMEM] * (1 + 2 * PIECES),
        scratch_shapes=[
            pltpu.VMEM((count, tokens, feat), BF16),
            pltpu.VMEM((count, tokens, feat), BF16),
            pltpu.VMEM((count, fresh, feat), BF16),
            pltpu.VMEM((count, fresh, feat), BF16),
            pltpu.VMEM((count, context, enc), BF16),
            pltpu.SemaphoreType.DMA((count, 2)),
            pltpu.SMEM((len(rows),), jnp.int32),
        ],
        out_shape=[row_shape, row_shape, turned_shape] + grad_shapes,
        input_output_aliases={aliased: 0, aliased + 1: 1} if carried else {},
        compiler_params=params(ATTEND_MIB),
        name="attend_blocks",
    )(own, *rows, *ready, wk, wv, queries, grad_out, *carried)


def weigh_kernel(chunks, carried, sides, *refs):
    refs = list(refs)
    take = lambda n: [refs.pop(0) for _ in range(n)]
    turned, grads = take(chunks), [take(chunks) for _ in range(2)]
    before = take(2) if carried else []
    enc = turned[0].shape[0]
    for side in sides:
        rows = slice(0, enc)
        if side is not None:
            half = lax.axis_index("dp") if side else 1 - lax.axis_index("dp")
            rows = pl.ds(pl.multiple_of(half * (enc // 2), enc // 2), enc // 2)
        for i in range(2):
            total = before[i][rows, :] if carried else 0.0
            for turn, ref in zip(turned, grads[i]):
                grad = ref[...]
                total += jnp.dot(turn[rows, :], grad.reshape(-1, grad.shape[-1]), preferred_element_type=F32)
            target = refs.pop(0)
            target[...] = total.astype(target.dtype)


def weigh(turned, dks, dvs, before, sides):
    enc, width = turned[0].shape[0], dks[0].shape[-1]
    shapes = [
        jax.ShapeDtypeStruct((enc, width), F32) if side is None else jax.ShapeDtypeStruct((enc // 2, width), BF16)
        for side in sides
        for _ in range(2)
    ]
    return pl.pallas_call(
        functools.partial(weigh_kernel, len(turned), bool(before), sides),
        in_specs=[VMEM] * (3 * len(turned) + len(before)),
        out_specs=[VMEM] * len(shapes),
        out_shape=shapes,
        compiler_params=params(WEIGH_MIB),
        name="weigh_grads",
    )(*turned, *dks, *dvs, *before)


def fold_kernel(dims, count, *refs):
    ret = lax.axis_index("ret")
    for i in range(count):
        held_ref, arrived_ref = refs[i], refs[count + i]
        bit, place = dims[i]
        mine = (ret >> bit) & 1
        stride = 1 << place
        for j in range(held_ref.shape[0] // 2):
            base = (j // stride) * 2 * stride + j % stride
            for k, side in enumerate((1 - mine, mine)):
                row = base + side * stride
                total = held_ref[row].astype(F32) + arrived_ref[row].astype(F32)
                refs[(2 + k) * count + i][j] = total.astype(BF16)


def fold(held, arrived, dims):
    count = len(held)
    parts, rows, width = held[0].shape
    shapes = [jax.ShapeDtypeStruct((parts // 2, rows, width), BF16)] * (2 * count)
    return pl.pallas_call(
        functools.partial(fold_kernel, dims, count),
        in_specs=[VMEM] * (2 * count),
        out_specs=[VMEM] * len(shapes),
        out_shape=shapes,
        compiler_params=params(16),
        name="fold_grads",
    )(*held, *arrived)


def join_kernel(*refs):
    count = (len(refs) - 2) // 2
    place = [0, 0]
    for i in range(count):
        total = refs[i][0].astype(F32) + refs[count + i][0].astype(F32)
        width = total.shape[1]
        refs[2 * count + i % 2][:, place[i % 2] : place[i % 2] + width] = total
        place[i % 2] += width


def join(held, arrived):
    rows, feat = held[0].shape[1], sum(part.shape[2] for part in held) // 2
    return pl.pallas_call(
        join_kernel,
        in_specs=[VMEM] * (2 * len(held)),
        out_specs=[VMEM] * 2,
        out_shape=[jax.ShapeDtypeStruct((rows, feat), F32)] * 2,
        compiler_params=params(16),
        name="join_grads",
    )(*held, *arrived)


class Sums:
    def __init__(self, send, held):
        self.bits = lax.axis_size("ret").bit_length() - 1
        self.left = [list(range(self.bits)) for _ in held]
        self.held = self.split(held)
        self.arrived = self.split([swap(grad, "dp", 1) for grad in send])
        self.steps = 0

    def split(self, grads):
        return [grad.reshape(1 << self.bits, -1, grad.shape[-1]) for grad in grads]

    def fold(self):
        self.bit = [self.steps, self.bits - 1 - self.steps]
        dims = tuple((bit, left.index(bit)) for bit, left in zip(self.bit, self.left))
        for bit, left in zip(self.bit, self.left):
            left.remove(bit)
        parts = fold(self.held, self.arrived, dims)
        self.send, self.held = list(parts[:2]), list(parts[2:])
        self.steps += 1

    def exchange(self):
        self.arrived = [swap(grad, "ret", 1 << bit) for grad, bit in zip(self.send, self.bit)]


def spans_of(blocks):
    spans, start = [], 0
    for count, pair in CHUNKS:
        spans.append((start, count, pair))
        start += count
    return spans if start == blocks else [(0, blocks, False)]


def local(queries, enc_states, w_key, w_value, shard_ids, row_ids, grad_out):
    n_ret = lax.axis_size("ret")
    blocks = shard_ids.shape[1]
    bound = blocks * NEIGHBOURS * 2 // n_ret
    enc = enc_states.shape[2]

    def capacity(count):
        return min(count, bound)

    own = jnp.stack([shard_ids[0], row_ids[0]], axis=-1).reshape(-1)
    ids = exchange_ids(own)
    normed = normalize_rows(enc_states[0]).reshape(-1, 2, HALF, enc)
    spans = spans_of(blocks)
    outgoing = pick(ids, normed, spans[:1], capacity)
    if len(spans) > 1:
        outgoing = outgoing + pick(ids, normed, spans[1:], capacity)
    query_blocks, grad_blocks = (array.reshape(blocks, -1, array.shape[2]) for array in (queries, grad_out))
    carried, arrivals = [], []
    for slots in outgoing:
        slots = list(slots)
        if arrivals:
            for k in range(1, n_ret):
                arrivals[-1][k], slots[k] = lax.optimization_barrier((arrivals[-1][k], slots[k]))
        arrivals.append(slots[:1] + [swap(slots[k], "ret", k) for k in range(1, n_ret)])
    rows, turned, found, sums, early = [None] * len(spans), [], [], [[]] * PIECES, None
    ready = [[] for _ in spans]

    def weigh_piece(turned, found, piece, before, sides):
        return list(weigh(turned, *([grads[2 * piece + i] for grads in found] for i in range(2)), before, sides))


    def prepare(i):
        start, count, pair = spans[i]
        if pair:
            mine = unpack(own, arrivals[i], start, count)
            rows[i] = [mine, swap(mine, "ctx", 1)]
            if PROJECT_FIRST:
                ready[i] = list(project(mine, w_key, w_value))
        else:
            rows[i] = arrivals[i]

    prepare(0)
    for i, (start, count, pair) in enumerate(spans):
        last = i + 1 == len(spans)
        if not last and spans[i + 1][2]:
            if ready[i]:
                ready[i][0], arrivals[i + 1] = lax.optimization_barrier((ready[i][0], arrivals[i + 1]))
            prepare(i + 1)
            rows[i][0], rows[i + 1][0] = lax.optimization_barrier((rows[i][0], rows[i + 1][0]))
        results = attend(rows[i], ready[i], own, w_key, w_value, query_blocks, grad_blocks, start, count, pair, carried)
        attended, grad_queries, flipped, *grads = results
        carried = [attended, grad_queries]
        turned.append(flipped)
        found.append(grads)
        if i == 0 and not last:
            early = turned, found
            turned, found = [], []
            sums[0] = weigh_piece(*early, 0, [], (None,))
            sums[0][0], rows[1][0] = lax.optimization_barrier((sums[0][0], rows[1][0]))
        if not last and rows[i + 1] is None:
            carried[0], arrivals[i + 1] = lax.optimization_barrier((carried[0], arrivals[i + 1]))
            prepare(i + 1)
    states = []
    for piece in range(PIECES):
        if piece:
            if early:
                parts[0], early[0][0] = lax.optimization_barrier((parts[0], early[0][0]))
                sums[piece] = weigh_piece(*early, piece, [], (None,))
            states.append(Sums(parts[:2], parts[2:]))
            states[-1].fold()
            states[-1].send, turned[0] = lax.optimization_barrier((states[-1].send, turned[0]))
        parts = []
        for sides in SIDES[piece]:
            parts += weigh_piece(turned, found, piece, sums[piece], sides)
    states.append(Sums(parts[:2], parts[2:]))
    states[-1].fold()
    for step in range(states[0].bits):
        for state in states:
            if step:
                state.fold()
            state.exchange()
    attended, grad_queries = carried
    grad_w_key, grad_w_value = join(sum([state.held for state in states], []), sum([state.arrived for state in states], []))
    return attended.reshape(queries.shape), grad_queries.reshape(queries.shape), grad_w_key, grad_w_value


def solution(mesh):
    placed = (
        P("dp", "ret", "ctx"),
        P("dp", "ret", None),
        P(None, "ctx"),
        P(None, "ctx"),
        P("dp", "ret", None),
        P("dp", "ret", None),
        P("dp", "ret", "ctx"),
    )
    return jax.shard_map(
        local,
        mesh=mesh,
        in_specs=placed,
        out_specs=(
            P("dp", "ret", "ctx"),
            P("dp", "ret", "ctx"),
            P(("dp", "ret"), "ctx"),
            P(("dp", "ret"), "ctx"),
        ),
        check_vma=False,
    )
```

```python
import functools
import math

import jax
import jax.numpy as jnp
from jax import lax
from jax.experimental import pallas as pl
from jax.experimental.pallas import tpu as pltpu
from jax.sharding import PartitionSpec as P

HEAD_DIM = 128
NEIGH_LEN = 128
NEIGHBOURS = 2
HALF = NEIGH_LEN // 2
MIB = 1024 * 1024
ATTEND_MIB = 26
WEIGH_MIB = 26
PIECES = 2
SIDES = (((False,), (True,)), ((False, True),))
PROJECT_FIRST = True
FIRST_PIECE = 6 / 8
CHUNKS = ((3, True), (3, True), (2, False))

F32 = jnp.float32
BF16 = jnp.bfloat16
ANY = pl.BlockSpec(memory_space=pl.ANY)
SMEM = pl.BlockSpec(memory_space=pltpu.SMEM)
VMEM = pl.BlockSpec(memory_space=pltpu.VMEM)
HBM = pl.BlockSpec(memory_space=pltpu.HBM)


def params(mib):
    return pltpu.CompilerParams(vmem_limit_bytes=mib * MIB)


def piece_heads(heads):
    return [0, int(heads * FIRST_PIECE), heads]


def contract(lhs, rhs, dims):
    return lax.dot_general(lhs, rhs, (dims, ((), ())), preferred_element_type=F32)


def swap(array, axis, bit):
    size = lax.axis_size(axis)
    return lax.ppermute(array, axis, [(i, i ^ bit) for i in range(size)])


def normalize_kernel(states_ref, out_ref):
    floats = states_ref[...].astype(F32)
    mean_square = jnp.mean(floats * floats, axis=-1, keepdims=True)
    out_ref[...] = (floats * lax.rsqrt(mean_square + 1e-06)).astype(BF16)


def normalize_rows(states):
    rows, width = states.shape
    tile = 512
    spec = pl.BlockSpec((tile, width), lambda i: (i, 0))
    return pl.pallas_call(
        normalize_kernel,
        grid=(rows // tile,),
        in_specs=[spec],
        out_specs=spec,
        out_shape=jax.ShapeDtypeStruct(states.shape, BF16),
        compiler_params=params(12),
        name="normalize_rows",
    )(states)


def exchange_ids(own):
    n_ret = lax.axis_size("ret")
    if n_ret <= 4:
        return jnp.stack([own] + [swap(own, "ret", k) for k in range(1, n_ret)])
    every = lax.all_gather(own, "ret")
    order = jnp.arange(n_ret, dtype=jnp.int32) ^ lax.axis_index("ret")
    return jnp.take(every, order, axis=0)


def pick_kernel(spans, id_ref, normed_ref, *outs):
    n_ret = id_ref.shape[0]
    me = lax.axis_index("ret")
    part = lax.rem(lax.axis_index("ctx"), 2)
    for chunk, (start, count, pair) in enumerate(spans):
        for k in range(n_ret):
            out_ref = outs[chunk * n_ret + k]

            def send(i, used, k=k, start=start, pair=pair, out_ref=out_ref):
                request = (start * NEIGHBOURS + i) * 2
                mine = id_ref[k, request] == me

                @pl.when(mine)
                def _():
                    row = id_ref[k, request + 1]
                    out_ref[used] = normed_ref[row, part] if pair else normed_ref[row]

                return used + jnp.where(mine, 1, 0)

            lax.fori_loop(0, count * NEIGHBOURS, send, jnp.int32(0))


def pick(ids, normed, spans, capacity):
    n_ret, width = ids.shape[0], normed.shape[-1]
    slots = [capacity(count) for _, count, _ in spans]
    shapes = [(cap, HALF, width) if pair else (cap, 2, HALF, width) for (_, _, pair), cap in zip(spans, slots)]
    shapes = [jax.ShapeDtypeStruct(shape, BF16) for shape in shapes for _ in range(n_ret)]
    picked = pl.pallas_call(
        functools.partial(pick_kernel, spans),
        in_specs=[SMEM, VMEM],
        out_specs=[VMEM] * len(shapes),
        out_shape=shapes,
        compiler_params=params(16),
        name="pick_rows",
    )(ids, normed)
    return [picked[i : i + n_ret] for i in range(0, len(picked), n_ret)]


def unpack_kernel(start, count, id_ref, *refs):
    *incoming, out_ref, ranks = refs
    place_rows(start, count, id_ref, incoming, ranks, lambda i: out_ref.at[i])


def place_rows(start, count, id_ref, incoming, ranks, target):
    me = lax.axis_index("ret")
    for k in range(len(incoming)):
        ranks[k] = 0
    for i in range(count * NEIGHBOURS):
        source = id_ref[(start * NEIGHBOURS + i) * 2] ^ me
        rank = ranks[source]
        ranks[source] = rank + 1
        for k in range(len(incoming)):

            @pl.when(source == k)
            def _(k=k, rank=rank, i=i):
                target(i)[...] = incoming[k][rank]


def unpack(own, incoming, start, count):
    return pl.pallas_call(
        functools.partial(unpack_kernel, start, count),
        in_specs=[SMEM] + [VMEM] * len(incoming),
        out_specs=VMEM,
        out_shape=jax.ShapeDtypeStruct((count * NEIGHBOURS,) + incoming[0].shape[1:], BF16),
        scratch_shapes=[pltpu.SMEM((len(incoming),), jnp.int32)],
        compiler_params=params(8),
        name="unpack_rows",
    )(own, *incoming)


def block_grads(keys, values, query, grad, out_ref, gq_ref, grad_refs):
    scale = 1.0 / math.sqrt(HEAD_DIM)
    tokens, heads = out_ref.shape[0], out_ref.shape[1] // HEAD_DIM
    zero = jnp.zeros((tokens, HEAD_DIM), BF16)
    bounds = piece_heads(heads)
    cols = [slice(head * HEAD_DIM, (head + 1) * HEAD_DIM) for head in range(heads)]

    def reader(head):
        upper = jnp.concatenate([query(cols[head]), zero], axis=1)
        lower = jnp.concatenate([zero, grad(cols[head])], axis=1)
        return jnp.concatenate([upper, lower], axis=0)

    def both(head):
        return jnp.concatenate([keys(cols[head]), values(cols[head])], axis=1)

    def finish(head, probs, dscore):
        mixed = jnp.dot(jnp.concatenate([probs, dscore], axis=0), both(head), preferred_element_type=F32)
        out_ref[:, cols[head]] = mixed[:tokens, HEAD_DIM:].astype(BF16)
        gq_ref[:, cols[head]] = mixed[tokens:, :HEAD_DIM].astype(BF16)
        grads = contract(jnp.concatenate([dscore, probs], axis=0), reader(head), ((0,), (0,))).astype(BF16)
        piece = int(head >= bounds[1])
        place = cols[head - bounds[piece]]
        grad_refs[2 * piece][:, place] = grads[:, :HEAD_DIM]
        grad_refs[2 * piece + 1][:, place] = grads[:, HEAD_DIM:]

    ahead, lag = 4, 3
    products, weights = {}, {}
    for head in range(-ahead, heads + lag):
        if 0 <= head + ahead < heads:
            products[head + ahead] = contract(reader(head + ahead), both(head + ahead), ((1,), (1,)))
        if 0 <= head < heads:
            product = products.pop(head)
            expo, dprob = jnp.exp(product[:tokens] * scale), product[tokens:]
            inverse = 1.0 / jnp.sum(expo, axis=-1, keepdims=True)
            delta = jnp.sum(expo * dprob, axis=-1, keepdims=True) * inverse
            probs = expo * inverse
            weights[head] = (probs.astype(BF16), (probs * (dprob - delta) * scale).astype(BF16))
        if 0 <= head - lag < heads:
            finish(head - lag, *weights.pop(head - lag))


def project_kernel(rows_ref, wk_ref, wv_ref, k_ref, v_ref):
    rows = rows_ref[...].reshape(-1, rows_ref.shape[-1])
    for w_ref, target in ((wk_ref, k_ref), (wv_ref, v_ref)):
        target[...] = jnp.dot(rows, w_ref[...], preferred_element_type=F32).astype(BF16).reshape(target.shape)


def project(rows, wk, wv):
    count, feat = rows.shape[0] // NEIGHBOURS, wk.shape[1]
    shape = jax.ShapeDtypeStruct((count, NEIGHBOURS * rows.shape[1], feat), BF16)
    return pl.pallas_call(
        project_kernel,
        in_specs=[VMEM] * 3,
        out_specs=[VMEM] * 2,
        out_shape=[shape] * 2,
        compiler_params=params(16),
        name="project_rows",
    )(rows, wk, wv)


def attend_kernel(start, count, sources, pair, done, id_ref, *refs):
    refs = list(refs)
    take = lambda n: [refs.pop(0) for _ in range(n)]
    row_refs = take(sources)
    ready = take(2 if done else 0)
    wk_ref, wv_ref, q_ref, go_ref = take(4)
    out_ref, gq_ref, turned = take(3)
    grad_refs = take(2 * PIECES)
    keys, values, rows, ranks = take(4)
    size, width = rows.shape[1:]
    part, feat = keys.shape[1:]
    if pair:
        for i, ref in enumerate(row_refs):
            rows[:, i * (size // 2) : (i + 1) * (size // 2)] = ref[...].reshape(count, size // 2, width)
    else:
        place_rows(start, count, id_ref, row_refs, ranks, lambda i: rows.at[i // NEIGHBOURS, pl.ds(i % NEIGHBOURS * NEIGH_LEN, NEIGH_LEN)])

    rest = (row_refs[1] if done else rows)[...].reshape(-1, width)
    for w_ref, target in ((wk_ref, keys), (wv_ref, values)):
        product = jnp.dot(rest, w_ref[...], preferred_element_type=F32).astype(BF16)
        target[...] = product.reshape(count, part, feat)

    def block(b, carry):
        def pick(at, *parts):
            return lambda cols: jnp.concatenate([ref[at, :, cols] for ref in parts], axis=0)

        context = pick(b, *ready[:1], keys), pick(b, *ready[1:], values)
        block_grads(*context, pick(start + b, q_ref), pick(start + b, go_ref), out_ref.at[b], gq_ref.at[b], [ref.at[b] for ref in grad_refs])
        return carry

    lax.fori_loop(0, count, block, 0)
    turned[...] = rows[...].reshape(-1, width).T


def attend(rows, ready, own, wk, wv, queries, grad_out, start, count, pair):
    _, tokens, feat = queries.shape
    enc = wk.shape[0]
    context = NEIGHBOURS * NEIGH_LEN
    row_shape = jax.ShapeDtypeStruct((count, tokens, feat), BF16)
    if not pair:
        rows = [part.reshape(part.shape[0], NEIGH_LEN, enc) for part in rows]
    turned_shape = jax.ShapeDtypeStruct((enc, count * context), BF16)
    bounds = piece_heads(feat // HEAD_DIM)
    widths = [(bounds[piece + 1] - bounds[piece]) * HEAD_DIM for piece in range(PIECES) for _ in range(2)]
    grad_shapes = [jax.ShapeDtypeStruct((count, context, width), BF16) for width in widths]
    fresh = context // 2 if ready else context
    settings = start, count, len(rows), pair, bool(ready)
    return pl.pallas_call(
        functools.partial(attend_kernel, *settings),
        in_specs=[SMEM] + [VMEM] * (len(rows) + len(ready) + 4),
        out_specs=[VMEM] * (3 + 2 * PIECES),
        scratch_shapes=[
            pltpu.VMEM((count, fresh, feat), BF16),
            pltpu.VMEM((count, fresh, feat), BF16),
            pltpu.VMEM((count, context, enc), BF16),
            pltpu.SMEM((len(rows),), jnp.int32),
        ],
        out_shape=[row_shape, row_shape, turned_shape] + grad_shapes,
        compiler_params=params(ATTEND_MIB),
        name="attend_blocks",
    )(own, *rows, *ready, wk, wv, queries, grad_out)


def weigh_kernel(chunks, carried, sides, *refs):
    refs = list(refs)
    take = lambda n: [refs.pop(0) for _ in range(n)]
    turned, grads = take(chunks), [take(chunks) for _ in range(2)]
    before = take(2) if carried else []
    enc = turned[0].shape[0]
    for side in sides:
        rows = slice(0, enc)
        if side is not None:
            half = lax.axis_index("dp") if side else 1 - lax.axis_index("dp")
            rows = pl.ds(pl.multiple_of(half * (enc // 2), enc // 2), enc // 2)
        for i in range(2):
            total = before[i][rows, :] if carried else 0.0
            for turn, ref in zip(turned, grads[i]):
                grad = ref[...]
                total += jnp.dot(turn[rows, :], grad.reshape(-1, grad.shape[-1]), preferred_element_type=F32)
            target = refs.pop(0)
            target[...] = total.astype(target.dtype)


def weigh(turned, dks, dvs, before, sides):
    enc, width = turned[0].shape[0], dks[0].shape[-1]
    shapes = [
        jax.ShapeDtypeStruct((enc, width), F32) if side is None else jax.ShapeDtypeStruct((enc // 2, width), BF16)
        for side in sides
        for _ in range(2)
    ]
    return pl.pallas_call(
        functools.partial(weigh_kernel, len(turned), bool(before), sides),
        in_specs=[VMEM] * (3 * len(turned) + len(before)),
        out_specs=[VMEM] * len(shapes),
        out_shape=shapes,
        compiler_params=params(WEIGH_MIB),
        name="weigh_grads",
    )(*turned, *dks, *dvs, *before)


def fold_kernel(dims, count, *refs):
    ret = lax.axis_index("ret")
    for i in range(count):
        held_ref, arrived_ref = refs[i], refs[count + i]
        bit, place = dims[i]
        mine = (ret >> bit) & 1
        stride = 1 << place
        for j in range(held_ref.shape[0] // 2):
            base = (j // stride) * 2 * stride + j % stride
            for k, side in enumerate((1 - mine, mine)):
                row = base + side * stride
                total = held_ref[row].astype(F32) + arrived_ref[row].astype(F32)
                refs[(2 + k) * count + i][j] = total.astype(BF16)


def fold(held, arrived, dims):
    count = len(held)
    parts, rows, width = held[0].shape
    shapes = [jax.ShapeDtypeStruct((parts // 2, rows, width), BF16)] * (2 * count)
    return pl.pallas_call(
        functools.partial(fold_kernel, dims, count),
        in_specs=[VMEM] * (2 * count),
        out_specs=[VMEM] * len(shapes),
        out_shape=shapes,
        compiler_params=params(16),
        name="fold_grads",
    )(*held, *arrived)


def join_kernel(*refs):
    count = (len(refs) - 2) // 2
    place = [0, 0]
    for i in range(count):
        total = refs[i][0].astype(F32) + refs[count + i][0].astype(F32)
        width = total.shape[1]
        refs[2 * count + i % 2][:, place[i % 2] : place[i % 2] + width] = total
        place[i % 2] += width


def join(held, arrived):
    rows, feat = held[0].shape[1], sum(part.shape[2] for part in held) // 2
    return pl.pallas_call(
        join_kernel,
        in_specs=[VMEM] * (2 * len(held)),
        out_specs=[VMEM] * 2,
        out_shape=[jax.ShapeDtypeStruct((rows, feat), F32)] * 2,
        compiler_params=params(16),
        name="join_grads",
    )(*held, *arrived)


class Sums:
    def __init__(self, send, held):
        self.bits = lax.axis_size("ret").bit_length() - 1
        self.left = [list(range(self.bits)) for _ in held]
        self.held = self.split(held)
        self.arrived = self.split([swap(grad, "dp", 1) for grad in send])
        self.steps = 0

    def split(self, grads):
        return [grad.reshape(1 << self.bits, -1, grad.shape[-1]) for grad in grads]

    def fold(self):
        self.bit = [self.steps, self.bits - 1 - self.steps]
        dims = tuple((bit, left.index(bit)) for bit, left in zip(self.bit, self.left))
        for bit, left in zip(self.bit, self.left):
            left.remove(bit)
        parts = fold(self.held, self.arrived, dims)
        self.send, self.held = list(parts[:2]), list(parts[2:])
        self.steps += 1

    def exchange(self):
        self.arrived = [swap(grad, "ret", 1 << bit) for grad, bit in zip(self.send, self.bit)]


def spans_of(blocks):
    spans, start = [], 0
    for count, pair in CHUNKS:
        spans.append((start, count, pair))
        start += count
    return spans if start == blocks else [(0, blocks, False)]


def local(queries, enc_states, w_key, w_value, shard_ids, row_ids, grad_out):
    n_ret = lax.axis_size("ret")
    blocks = shard_ids.shape[1]
    bound = blocks * NEIGHBOURS * 2 // n_ret
    enc = enc_states.shape[2]

    def capacity(count):
        return min(count, bound)

    own = jnp.stack([shard_ids[0], row_ids[0]], axis=-1).reshape(-1)
    ids = exchange_ids(own)
    normed = normalize_rows(enc_states[0]).reshape(-1, 2, HALF, enc)
    spans = spans_of(blocks)
    outgoing = pick(ids, normed, spans[:1], capacity)
    if len(spans) > 1:
        outgoing = outgoing + pick(ids, normed, spans[1:], capacity)
    query_blocks, grad_blocks = (array.reshape(blocks, -1, array.shape[2]) for array in (queries, grad_out))
    attended, grad_queries, arrivals = [], [], []
    for slots in outgoing:
        slots = list(slots)
        if arrivals:
            for k in range(1, n_ret):
                arrivals[-1][k], slots[k] = lax.optimization_barrier((arrivals[-1][k], slots[k]))
        arrivals.append(slots[:1] + [swap(slots[k], "ret", k) for k in range(1, n_ret)])
    rows, turned, found, sums, early = [None] * len(spans), [], [], [[]] * PIECES, None
    ready = [[] for _ in spans]

    def weigh_piece(turned, found, piece, before, sides):
        return list(weigh(turned, *([grads[2 * piece + i] for grads in found] for i in range(2)), before, sides))


    def prepare(i):
        start, count, pair = spans[i]
        if pair:
            mine = unpack(own, arrivals[i], start, count)
            rows[i] = [mine, swap(mine, "ctx", 1)]
            if PROJECT_FIRST:
                ready[i] = list(project(mine, w_key, w_value))
        else:
            rows[i] = arrivals[i]

    prepare(0)
    for i, (start, count, pair) in enumerate(spans):
        last = i + 1 == len(spans)
        if not last and spans[i + 1][2]:
            if ready[i]:
                ready[i][0], arrivals[i + 1] = lax.optimization_barrier((ready[i][0], arrivals[i + 1]))
            prepare(i + 1)
            rows[i][0], rows[i + 1][0] = lax.optimization_barrier((rows[i][0], rows[i + 1][0]))
        results = attend(rows[i], ready[i], own, w_key, w_value, query_blocks, grad_blocks, start, count, pair)
        out, gq, flipped, *grads = results
        attended.append(out)
        grad_queries.append(gq)
        turned.append(flipped)
        found.append(grads)
        if i == 0 and not last:
            early = turned, found
            turned, found = [], []
            sums[0] = weigh_piece(*early, 0, [], (None,))
            sums[0][0], rows[1][0] = lax.optimization_barrier((sums[0][0], rows[1][0]))
        if not last and rows[i + 1] is None:
            attended[-1], arrivals[i + 1] = lax.optimization_barrier((attended[-1], arrivals[i + 1]))
            prepare(i + 1)
    states = []
    for piece in range(PIECES):
        if piece:
            if early:
                parts[0], early[0][0] = lax.optimization_barrier((parts[0], early[0][0]))
                sums[piece] = weigh_piece(*early, piece, [], (None,))
            states.append(Sums(parts[:2], parts[2:]))
            states[-1].fold()
            states[-1].send, turned[0] = lax.optimization_barrier((states[-1].send, turned[0]))
        parts = []
        for sides in SIDES[piece]:
            parts += weigh_piece(turned, found, piece, sums[piece], sides)
    states.append(Sums(parts[:2], parts[2:]))
    states[-1].fold()
    for step in range(states[0].bits):
        for state in states:
            if step:
                state.fold()
            state.exchange()
    grad_w_key, grad_w_value = join(sum([state.held for state in states], []), sum([state.arrived for state in states], []))
    attended, grad_queries = (jnp.concatenate(blocks).reshape(queries.shape) for blocks in (attended, grad_queries))
    return attended, grad_queries, grad_w_key, grad_w_value


def solution(mesh):
    placed = (
        P("dp", "ret", "ctx"),
        P("dp", "ret", None),
        P(None, "ctx"),
        P(None, "ctx"),
        P("dp", "ret", None),
        P("dp", "ret", None),
        P("dp", "ret", "ctx"),
    )
    return jax.shard_map(
        local,
        mesh=mesh,
        in_specs=placed,
        out_specs=(
            P("dp", "ret", "ctx"),
            P("dp", "ret", "ctx"),
            P(("dp", "ret"), "ctx"),
            P(("dp", "ret"), "ctx"),
        ),
        check_vma=False,
    )
```

```python
import functools
import math

import jax
import jax.numpy as jnp
from jax import lax
from jax.experimental import pallas as pl
from jax.experimental.pallas import tpu as pltpu
from jax.sharding import PartitionSpec as P

HEAD_DIM = 128
NEIGH_LEN = 128
NEIGHBOURS = 2
HALF = NEIGH_LEN // 2
MIB = 1024 * 1024
ATTEND_MIB = 26
WEIGH_MIB = 26
PIECES = 2
SIDES = ((((False,), (0,)), ((False,), (1,)), ((True,), (0, 1))), (((False, True), (0, 1)),))
PROJECT_FIRST = True
FIRST_PIECE = 6 / 8
CHUNKS = ((3, True), (3, True), (2, False))

F32 = jnp.float32
BF16 = jnp.bfloat16
ANY = pl.BlockSpec(memory_space=pl.ANY)
SMEM = pl.BlockSpec(memory_space=pltpu.SMEM)
VMEM = pl.BlockSpec(memory_space=pltpu.VMEM)
HBM = pl.BlockSpec(memory_space=pltpu.HBM)


def params(mib):
    return pltpu.CompilerParams(vmem_limit_bytes=mib * MIB)


def piece_heads(heads):
    return [0, int(heads * FIRST_PIECE), heads]


def contract(lhs, rhs, dims):
    return lax.dot_general(lhs, rhs, (dims, ((), ())), preferred_element_type=F32)


def swap(array, axis, bit):
    size = lax.axis_size(axis)
    return lax.ppermute(array, axis, [(i, i ^ bit) for i in range(size)])


def normalize_kernel(states_ref, out_ref):
    floats = states_ref[...].astype(F32)
    mean_square = jnp.mean(floats * floats, axis=-1, keepdims=True)
    out_ref[...] = (floats * lax.rsqrt(mean_square + 1e-06)).astype(BF16)


def normalize_rows(states):
    rows, width = states.shape
    tile = 512
    spec = pl.BlockSpec((tile, width), lambda i: (i, 0))
    return pl.pallas_call(
        normalize_kernel,
        grid=(rows // tile,),
        in_specs=[spec],
        out_specs=spec,
        out_shape=jax.ShapeDtypeStruct(states.shape, BF16),
        compiler_params=params(12),
        name="normalize_rows",
    )(states)


def exchange_ids(own):
    n_ret = lax.axis_size("ret")
    if n_ret <= 4:
        return jnp.stack([own] + [swap(own, "ret", k) for k in range(1, n_ret)])
    every = lax.all_gather(own, "ret")
    order = jnp.arange(n_ret, dtype=jnp.int32) ^ lax.axis_index("ret")
    return jnp.take(every, order, axis=0)


def pick_kernel(spans, id_ref, normed_ref, *outs):
    n_ret = id_ref.shape[0]
    me = lax.axis_index("ret")
    part = lax.rem(lax.axis_index("ctx"), 2)
    for chunk, (start, count, pair) in enumerate(spans):
        for k in range(n_ret):
            out_ref = outs[chunk * n_ret + k]

            def send(i, used, k=k, start=start, pair=pair, out_ref=out_ref):
                request = (start * NEIGHBOURS + i) * 2
                mine = id_ref[k, request] == me

                @pl.when(mine)
                def _():
                    row = id_ref[k, request + 1]
                    out_ref[used] = normed_ref[row, part] if pair else normed_ref[row]

                return used + jnp.where(mine, 1, 0)

            lax.fori_loop(0, count * NEIGHBOURS, send, jnp.int32(0))


def pick(ids, normed, spans, capacity):
    n_ret, width = ids.shape[0], normed.shape[-1]
    slots = [capacity(count) for _, count, _ in spans]
    shapes = [(cap, HALF, width) if pair else (cap, 2, HALF, width) for (_, _, pair), cap in zip(spans, slots)]
    shapes = [jax.ShapeDtypeStruct(shape, BF16) for shape in shapes for _ in range(n_ret)]
    picked = pl.pallas_call(
        functools.partial(pick_kernel, spans),
        in_specs=[SMEM, VMEM],
        out_specs=[VMEM] * len(shapes),
        out_shape=shapes,
        compiler_params=params(16),
        name="pick_rows",
    )(ids, normed)
    return [picked[i : i + n_ret] for i in range(0, len(picked), n_ret)]


def unpack_kernel(start, count, id_ref, *refs):
    *incoming, out_ref, ranks = refs
    place_rows(start, count, id_ref, incoming, ranks, lambda i: out_ref.at[i])


def place_rows(start, count, id_ref, incoming, ranks, target):
    me = lax.axis_index("ret")
    for k in range(len(incoming)):
        ranks[k] = 0
    for i in range(count * NEIGHBOURS):
        source = id_ref[(start * NEIGHBOURS + i) * 2] ^ me
        rank = ranks[source]
        ranks[source] = rank + 1
        for k in range(len(incoming)):

            @pl.when(source == k)
            def _(k=k, rank=rank, i=i):
                target(i)[...] = incoming[k][rank]


def unpack(own, incoming, start, count):
    return pl.pallas_call(
        functools.partial(unpack_kernel, start, count),
        in_specs=[SMEM] + [VMEM] * len(incoming),
        out_specs=VMEM,
        out_shape=jax.ShapeDtypeStruct((count * NEIGHBOURS,) + incoming[0].shape[1:], BF16),
        scratch_shapes=[pltpu.SMEM((len(incoming),), jnp.int32)],
        compiler_params=params(8),
        name="unpack_rows",
    )(own, *incoming)


def block_grads(keys, values, query, grad, out_ref, gq_ref, grad_refs):
    scale = 1.0 / math.sqrt(HEAD_DIM)
    tokens, heads = out_ref.shape[0], out_ref.shape[1] // HEAD_DIM
    zero = jnp.zeros((tokens, HEAD_DIM), BF16)
    bounds = piece_heads(heads)
    cols = [slice(head * HEAD_DIM, (head + 1) * HEAD_DIM) for head in range(heads)]

    def reader(head):
        upper = jnp.concatenate([query(cols[head]), zero], axis=1)
        lower = jnp.concatenate([zero, grad(cols[head])], axis=1)
        return jnp.concatenate([upper, lower], axis=0)

    def both(head):
        return jnp.concatenate([keys(cols[head]), values(cols[head])], axis=1)

    def finish(head, probs, dscore):
        mixed = jnp.dot(jnp.concatenate([probs, dscore], axis=0), both(head), preferred_element_type=F32)
        out_ref[:, cols[head]] = mixed[:tokens, HEAD_DIM:].astype(BF16)
        gq_ref[:, cols[head]] = mixed[tokens:, :HEAD_DIM].astype(BF16)
        grads = contract(jnp.concatenate([dscore, probs], axis=0), reader(head), ((0,), (0,))).astype(BF16)
        piece = int(head >= bounds[1])
        place = cols[head - bounds[piece]]
        grad_refs[2 * piece][:, place] = grads[:, :HEAD_DIM]
        grad_refs[2 * piece + 1][:, place] = grads[:, HEAD_DIM:]

    ahead, lag = 4, 3
    products, weights = {}, {}
    for head in range(-ahead, heads + lag):
        if 0 <= head + ahead < heads:
            products[head + ahead] = contract(reader(head + ahead), both(head + ahead), ((1,), (1,)))
        if 0 <= head < heads:
            product = products.pop(head)
            expo, dprob = jnp.exp(product[:tokens] * scale), product[tokens:]
            inverse = 1.0 / jnp.sum(expo, axis=-1, keepdims=True)
            delta = jnp.sum(expo * dprob, axis=-1, keepdims=True) * inverse
            probs = expo * inverse
            weights[head] = (probs.astype(BF16), (probs * (dprob - delta) * scale).astype(BF16))
        if 0 <= head - lag < heads:
            finish(head - lag, *weights.pop(head - lag))


def project_kernel(rows_ref, wk_ref, wv_ref, k_ref, v_ref):
    rows = rows_ref[...].reshape(-1, rows_ref.shape[-1])
    for w_ref, target in ((wk_ref, k_ref), (wv_ref, v_ref)):
        target[...] = jnp.dot(rows, w_ref[...], preferred_element_type=F32).astype(BF16).reshape(target.shape)


def project(rows, wk, wv):
    count, feat = rows.shape[0] // NEIGHBOURS, wk.shape[1]
    shape = jax.ShapeDtypeStruct((count, NEIGHBOURS * rows.shape[1], feat), BF16)
    return pl.pallas_call(
        project_kernel,
        in_specs=[VMEM] * 3,
        out_specs=[VMEM] * 2,
        out_shape=[shape] * 2,
        compiler_params=params(16),
        name="project_rows",
    )(rows, wk, wv)


def attend_kernel(start, count, sources, pair, done, id_ref, *refs):
    refs = list(refs)
    take = lambda n: [refs.pop(0) for _ in range(n)]
    row_refs = take(sources)
    ready = take(2 if done else 0)
    wk_ref, wv_ref, q_ref, go_ref = take(4)
    out_ref, gq_ref, turned = take(3)
    grad_refs = take(2 * PIECES)
    keys, values, rows, ranks = take(4)
    size, width = rows.shape[1:]
    part, feat = keys.shape[1:]
    if pair:
        for i, ref in enumerate(row_refs):
            rows[:, i * (size // 2) : (i + 1) * (size // 2)] = ref[...].reshape(count, size // 2, width)
    else:
        place_rows(start, count, id_ref, row_refs, ranks, lambda i: rows.at[i // NEIGHBOURS, pl.ds(i % NEIGHBOURS * NEIGH_LEN, NEIGH_LEN)])

    rest = (row_refs[1] if done else rows)[...].reshape(-1, width)
    for w_ref, target in ((wk_ref, keys), (wv_ref, values)):
        product = jnp.dot(rest, w_ref[...], preferred_element_type=F32).astype(BF16)
        target[...] = product.reshape(count, part, feat)

    def block(b, carry):
        def pick(at, *parts):
            return lambda cols: jnp.concatenate([ref[at, :, cols] for ref in parts], axis=0)

        context = pick(b, *ready[:1], keys), pick(b, *ready[1:], values)
        block_grads(*context, pick(start + b, q_ref), pick(start + b, go_ref), out_ref.at[b], gq_ref.at[b], [ref.at[b] for ref in grad_refs])
        return carry

    lax.fori_loop(0, count, block, 0)
    turned[...] = rows[...].reshape(-1, width).T


def attend(rows, ready, own, wk, wv, queries, grad_out, start, count, pair):
    _, tokens, feat = queries.shape
    enc = wk.shape[0]
    context = NEIGHBOURS * NEIGH_LEN
    row_shape = jax.ShapeDtypeStruct((count, tokens, feat), BF16)
    if not pair:
        rows = [part.reshape(part.shape[0], NEIGH_LEN, enc) for part in rows]
    turned_shape = jax.ShapeDtypeStruct((enc, count * context), BF16)
    bounds = piece_heads(feat // HEAD_DIM)
    widths = [(bounds[piece + 1] - bounds[piece]) * HEAD_DIM for piece in range(PIECES) for _ in range(2)]
    grad_shapes = [jax.ShapeDtypeStruct((count, context, width), BF16) for width in widths]
    fresh = context // 2 if ready else context
    settings = start, count, len(rows), pair, bool(ready)
    return pl.pallas_call(
        functools.partial(attend_kernel, *settings),
        in_specs=[SMEM] + [VMEM] * (len(rows) + len(ready) + 4),
        out_specs=[VMEM] * (3 + 2 * PIECES),
        scratch_shapes=[
            pltpu.VMEM((count, fresh, feat), BF16),
            pltpu.VMEM((count, fresh, feat), BF16),
            pltpu.VMEM((count, context, enc), BF16),
            pltpu.SMEM((len(rows),), jnp.int32),
        ],
        out_shape=[row_shape, row_shape, turned_shape] + grad_shapes,
        compiler_params=params(ATTEND_MIB),
        name="attend_blocks",
    )(own, *rows, *ready, wk, wv, queries, grad_out)


def weigh_kernel(chunks, streams, carried, sides, *refs):
    refs = list(refs)
    take = lambda n: [refs.pop(0) for _ in range(n)]
    turned, grads = take(chunks), [take(chunks) for _ in range(streams)]
    before = take(streams) if carried else []
    enc = turned[0].shape[0]
    for side in sides:
        rows = slice(0, enc)
        if side is not None:
            half = lax.axis_index("dp") if side else 1 - lax.axis_index("dp")
            rows = pl.ds(pl.multiple_of(half * (enc // 2), enc // 2), enc // 2)
        for i in range(streams):
            total = before[i][rows, :] if carried else 0.0
            for turn, ref in zip(turned, grads[i]):
                grad = ref[...]
                total += jnp.dot(turn[rows, :], grad.reshape(-1, grad.shape[-1]), preferred_element_type=F32)
            target = refs.pop(0)
            target[...] = total.astype(target.dtype)


def weigh(turned, grads, before, sides):
    enc, width = turned[0].shape[0], grads[0][0].shape[-1]
    shapes = [
        jax.ShapeDtypeStruct((enc, width), F32) if side is None else jax.ShapeDtypeStruct((enc // 2, width), BF16)
        for side in sides
        for _ in grads
    ]
    return pl.pallas_call(
        functools.partial(weigh_kernel, len(turned), len(grads), bool(before), sides),
        in_specs=[VMEM] * ((1 + len(grads)) * len(turned) + len(before)),
        out_specs=[VMEM] * len(shapes),
        out_shape=shapes,
        compiler_params=params(WEIGH_MIB),
        name="weigh_grads",
    )(*turned, *sum(grads, []), *before)


def fold_kernel(dims, count, *refs):
    ret = lax.axis_index("ret")
    for i in range(count):
        held_ref, arrived_ref = refs[i], refs[count + i]
        bit, place = dims[i]
        mine = (ret >> bit) & 1
        stride = 1 << place
        for j in range(held_ref.shape[0] // 2):
            base = (j // stride) * 2 * stride + j % stride
            for k, side in enumerate((1 - mine, mine)):
                row = base + side * stride
                total = held_ref[row].astype(F32) + arrived_ref[row].astype(F32)
                refs[(2 + k) * count + i][j] = total.astype(BF16)


def fold(held, arrived, dims):
    count = len(held)
    parts, rows, width = held[0].shape
    shapes = [jax.ShapeDtypeStruct((parts // 2, rows, width), BF16)] * (2 * count)
    return pl.pallas_call(
        functools.partial(fold_kernel, dims, count),
        in_specs=[VMEM] * (2 * count),
        out_specs=[VMEM] * len(shapes),
        out_shape=shapes,
        compiler_params=params(16),
        name="fold_grads",
    )(*held, *arrived)


def join_kernel(*refs):
    count = (len(refs) - 2) // 2
    place = [0, 0]
    for i in range(count):
        total = refs[i][0].astype(F32) + refs[count + i][0].astype(F32)
        width = total.shape[1]
        refs[2 * count + i % 2][:, place[i % 2] : place[i % 2] + width] = total
        place[i % 2] += width


def join(held, arrived):
    rows, feat = held[0].shape[1], sum(part.shape[2] for part in held) // 2
    return pl.pallas_call(
        join_kernel,
        in_specs=[VMEM] * (2 * len(held)),
        out_specs=[VMEM] * 2,
        out_shape=[jax.ShapeDtypeStruct((rows, feat), F32)] * 2,
        compiler_params=params(16),
        name="join_grads",
    )(*held, *arrived)


class Sums:
    def __init__(self, send, held):
        self.bits = lax.axis_size("ret").bit_length() - 1
        self.left = [list(range(self.bits)) for _ in held]
        self.held = self.split(held)
        self.arrived = self.split([swap(grad, "dp", 1) for grad in send])
        self.steps = 0

    def split(self, grads):
        return [grad.reshape(1 << self.bits, -1, grad.shape[-1]) for grad in grads]

    def fold(self):
        self.bit = [self.steps, self.bits - 1 - self.steps]
        dims = tuple((bit, left.index(bit)) for bit, left in zip(self.bit, self.left))
        for bit, left in zip(self.bit, self.left):
            left.remove(bit)
        parts = fold(self.held, self.arrived, dims)
        self.send, self.held = list(parts[:2]), list(parts[2:])
        self.steps += 1

    def exchange(self):
        self.arrived = [swap(grad, "ret", 1 << bit) for grad, bit in zip(self.send, self.bit)]


def spans_of(blocks):
    spans, start = [], 0
    for count, pair in CHUNKS:
        spans.append((start, count, pair))
        start += count
    return spans if start == blocks else [(0, blocks, False)]


def local(queries, enc_states, w_key, w_value, shard_ids, row_ids, grad_out):
    n_ret = lax.axis_size("ret")
    blocks = shard_ids.shape[1]
    bound = blocks * NEIGHBOURS * 2 // n_ret
    enc = enc_states.shape[2]

    def capacity(count):
        return min(count, bound)

    own = jnp.stack([shard_ids[0], row_ids[0]], axis=-1).reshape(-1)
    ids = exchange_ids(own)
    normed = normalize_rows(enc_states[0]).reshape(-1, 2, HALF, enc)
    spans = spans_of(blocks)
    outgoing = pick(ids, normed, spans[:1], capacity)
    if len(spans) > 1:
        outgoing = outgoing + pick(ids, normed, spans[1:], capacity)
    query_blocks, grad_blocks = (array.reshape(blocks, -1, array.shape[2]) for array in (queries, grad_out))
    attended, grad_queries, arrivals = [], [], []
    for slots in outgoing:
        slots = list(slots)
        if arrivals:
            for k in range(1, n_ret):
                arrivals[-1][k], slots[k] = lax.optimization_barrier((arrivals[-1][k], slots[k]))
        arrivals.append(slots[:1] + [swap(slots[k], "ret", k) for k in range(1, n_ret)])
    rows, turned, found, sums, early = [None] * len(spans), [], [], [[]] * PIECES, None
    ready = [[] for _ in spans]

    def weigh_piece(turned, found, piece, before, sides, streams=(0, 1)):
        before = [before[i] for i in streams] if before else []
        return list(weigh(turned, [[grads[2 * piece + i] for grads in found] for i in streams], before, sides))


    def prepare(i):
        start, count, pair = spans[i]
        if pair:
            mine = unpack(own, arrivals[i], start, count)
            rows[i] = [mine, swap(mine, "ctx", 1)]
            if PROJECT_FIRST:
                ready[i] = list(project(mine, w_key, w_value))
        else:
            rows[i] = arrivals[i]

    prepare(0)
    for i, (start, count, pair) in enumerate(spans):
        last = i + 1 == len(spans)
        if not last and spans[i + 1][2]:
            if ready[i]:
                ready[i][0], arrivals[i + 1] = lax.optimization_barrier((ready[i][0], arrivals[i + 1]))
            prepare(i + 1)
            rows[i][0], rows[i + 1][0] = lax.optimization_barrier((rows[i][0], rows[i + 1][0]))
        results = attend(rows[i], ready[i], own, w_key, w_value, query_blocks, grad_blocks, start, count, pair)
        out, gq, flipped, *grads = results
        attended.append(out)
        grad_queries.append(gq)
        turned.append(flipped)
        found.append(grads)
        if i == 0 and not last:
            early = turned, found
            turned, found = [], []
            sums[0] = weigh_piece(*early, 0, [], (None,))
            sums[0][0], rows[1][0] = lax.optimization_barrier((sums[0][0], rows[1][0]))
        if not last and rows[i + 1] is None:
            attended[-1], arrivals[i + 1] = lax.optimization_barrier((attended[-1], arrivals[i + 1]))
            prepare(i + 1)
    states = []
    for piece in range(PIECES):
        if piece:
            if early:
                parts[0], early[0][0] = lax.optimization_barrier((parts[0], early[0][0]))
                sums[piece] = weigh_piece(*early, piece, [], (None,))
            states.append(Sums(parts[:2], parts[2:]))
            states[-1].fold()
            states[-1].send, turned[0] = lax.optimization_barrier((states[-1].send, turned[0]))
        parts = []
        for sides, streams in SIDES[piece]:
            parts += weigh_piece(turned, found, piece, sums[piece], sides, streams)
    states.append(Sums(parts[:2], parts[2:]))
    states[-1].fold()
    for step in range(states[0].bits):
        for state in states:
            if step:
                state.fold()
            state.exchange()
    grad_w_key, grad_w_value = join(sum([state.held for state in states], []), sum([state.arrived for state in states], []))
    attended, grad_queries = (jnp.concatenate(blocks).reshape(queries.shape) for blocks in (attended, grad_queries))
    return attended, grad_queries, grad_w_key, grad_w_value


def solution(mesh):
    placed = (
        P("dp", "ret", "ctx"),
        P("dp", "ret", None),
        P(None, "ctx"),
        P(None, "ctx"),
        P("dp", "ret", None),
        P("dp", "ret", None),
        P("dp", "ret", "ctx"),
    )
    return jax.shard_map(
        local,
        mesh=mesh,
        in_specs=placed,
        out_specs=(
            P("dp", "ret", "ctx"),
            P("dp", "ret", "ctx"),
            P(("dp", "ret"), "ctx"),
            P(("dp", "ret"), "ctx"),
        ),
        check_vma=False,
    )
```

```python
import functools
import math

import jax
import jax.numpy as jnp
from jax import lax
from jax.experimental import pallas as pl
from jax.experimental.pallas import tpu as pltpu
from jax.sharding import PartitionSpec as P

HEAD_DIM = 128
NEIGH_LEN = 128
NEIGHBOURS = 2
HALF = NEIGH_LEN // 2
MIB = 1024 * 1024
ATTEND_MIB = 26
WEIGH_MIB = 26
PIECES = 2
SIDES = ((((False,), (0,)), ((False,), (1,)), ((True,), (0,)), ((True,), (1,))), (((False, True), (0, 1)),))
PROJECT_FIRST = True
FIRST_PIECE = 6 / 8
CHUNKS = ((3, True), (3, True), (2, False))

F32 = jnp.float32
BF16 = jnp.bfloat16
ANY = pl.BlockSpec(memory_space=pl.ANY)
SMEM = pl.BlockSpec(memory_space=pltpu.SMEM)
VMEM = pl.BlockSpec(memory_space=pltpu.VMEM)
HBM = pl.BlockSpec(memory_space=pltpu.HBM)


def params(mib):
    return pltpu.CompilerParams(vmem_limit_bytes=mib * MIB)


def piece_heads(heads):
    return [0, int(heads * FIRST_PIECE), heads]


def contract(lhs, rhs, dims):
    return lax.dot_general(lhs, rhs, (dims, ((), ())), preferred_element_type=F32)


def swap(array, axis, bit):
    size = lax.axis_size(axis)
    return lax.ppermute(array, axis, [(i, i ^ bit) for i in range(size)])


def normalize_kernel(states_ref, out_ref):
    floats = states_ref[...].astype(F32)
    mean_square = jnp.mean(floats * floats, axis=-1, keepdims=True)
    out_ref[...] = (floats * lax.rsqrt(mean_square + 1e-06)).astype(BF16)


def normalize_rows(states):
    rows, width = states.shape
    tile = 512
    spec = pl.BlockSpec((tile, width), lambda i: (i, 0))
    return pl.pallas_call(
        normalize_kernel,
        grid=(rows // tile,),
        in_specs=[spec],
        out_specs=spec,
        out_shape=jax.ShapeDtypeStruct(states.shape, BF16),
        compiler_params=params(12),
        name="normalize_rows",
    )(states)


def exchange_ids(own):
    n_ret = lax.axis_size("ret")
    if n_ret <= 4:
        return jnp.stack([own] + [swap(own, "ret", k) for k in range(1, n_ret)])
    every = lax.all_gather(own, "ret")
    order = jnp.arange(n_ret, dtype=jnp.int32) ^ lax.axis_index("ret")
    return jnp.take(every, order, axis=0)


def pick_kernel(spans, id_ref, normed_ref, *outs):
    n_ret = id_ref.shape[0]
    me = lax.axis_index("ret")
    part = lax.rem(lax.axis_index("ctx"), 2)
    for chunk, (start, count, pair) in enumerate(spans):
        for k in range(n_ret):
            out_ref = outs[chunk * n_ret + k]

            def send(i, used, k=k, start=start, pair=pair, out_ref=out_ref):
                request = (start * NEIGHBOURS + i) * 2
                mine = id_ref[k, request] == me

                @pl.when(mine)
                def _():
                    row = id_ref[k, request + 1]
                    out_ref[used] = normed_ref[row, part] if pair else normed_ref[row]

                return used + jnp.where(mine, 1, 0)

            lax.fori_loop(0, count * NEIGHBOURS, send, jnp.int32(0))


def pick(ids, normed, spans, capacity):
    n_ret, width = ids.shape[0], normed.shape[-1]
    slots = [capacity(count) for _, count, _ in spans]
    shapes = [(cap, HALF, width) if pair else (cap, 2, HALF, width) for (_, _, pair), cap in zip(spans, slots)]
    shapes = [jax.ShapeDtypeStruct(shape, BF16) for shape in shapes for _ in range(n_ret)]
    picked = pl.pallas_call(
        functools.partial(pick_kernel, spans),
        in_specs=[SMEM, VMEM],
        out_specs=[VMEM] * len(shapes),
        out_shape=shapes,
        compiler_params=params(16),
        name="pick_rows",
    )(ids, normed)
    return [picked[i : i + n_ret] for i in range(0, len(picked), n_ret)]


def unpack_kernel(start, count, id_ref, *refs):
    *incoming, out_ref, ranks = refs
    place_rows(start, count, id_ref, incoming, ranks, lambda i: out_ref.at[i])


def place_rows(start, count, id_ref, incoming, ranks, target):
    me = lax.axis_index("ret")
    for k in range(len(incoming)):
        ranks[k] = 0
    for i in range(count * NEIGHBOURS):
        source = id_ref[(start * NEIGHBOURS + i) * 2] ^ me
        rank = ranks[source]
        ranks[source] = rank + 1
        for k in range(len(incoming)):

            @pl.when(source == k)
            def _(k=k, rank=rank, i=i):
                target(i)[...] = incoming[k][rank]


def unpack(own, incoming, start, count):
    return pl.pallas_call(
        functools.partial(unpack_kernel, start, count),
        in_specs=[SMEM] + [VMEM] * len(incoming),
        out_specs=VMEM,
        out_shape=jax.ShapeDtypeStruct((count * NEIGHBOURS,) + incoming[0].shape[1:], BF16),
        scratch_shapes=[pltpu.SMEM((len(incoming),), jnp.int32)],
        compiler_params=params(8),
        name="unpack_rows",
    )(own, *incoming)


def block_grads(keys, values, query, grad, out_ref, gq_ref, grad_refs):
    scale = 1.0 / math.sqrt(HEAD_DIM)
    tokens, heads = out_ref.shape[0], out_ref.shape[1] // HEAD_DIM
    zero = jnp.zeros((tokens, HEAD_DIM), BF16)
    bounds = piece_heads(heads)
    cols = [slice(head * HEAD_DIM, (head + 1) * HEAD_DIM) for head in range(heads)]

    def reader(head):
        upper = jnp.concatenate([query(cols[head]), zero], axis=1)
        lower = jnp.concatenate([zero, grad(cols[head])], axis=1)
        return jnp.concatenate([upper, lower], axis=0)

    def both(head):
        return jnp.concatenate([keys(cols[head]), values(cols[head])], axis=1)

    def finish(head, probs, dscore):
        mixed = jnp.dot(jnp.concatenate([probs, dscore], axis=0), both(head), preferred_element_type=F32)
        out_ref[:, cols[head]] = mixed[:tokens, HEAD_DIM:].astype(BF16)
        gq_ref[:, cols[head]] = mixed[tokens:, :HEAD_DIM].astype(BF16)
        grads = contract(jnp.concatenate([dscore, probs], axis=0), reader(head), ((0,), (0,))).astype(BF16)
        piece = int(head >= bounds[1])
        place = cols[head - bounds[piece]]
        grad_refs[2 * piece][:, place] = grads[:, :HEAD_DIM]
        grad_refs[2 * piece + 1][:, place] = grads[:, HEAD_DIM:]

    ahead, lag = 4, 3
    products, weights = {}, {}
    for head in range(-ahead, heads + lag):
        if 0 <= head + ahead < heads:
            products[head + ahead] = contract(reader(head + ahead), both(head + ahead), ((1,), (1,)))
        if 0 <= head < heads:
            product = products.pop(head)
            expo, dprob = jnp.exp(product[:tokens] * scale), product[tokens:]
            inverse = 1.0 / jnp.sum(expo, axis=-1, keepdims=True)
            delta = jnp.sum(expo * dprob, axis=-1, keepdims=True) * inverse
            probs = expo * inverse
            weights[head] = (probs.astype(BF16), (probs * (dprob - delta) * scale).astype(BF16))
        if 0 <= head - lag < heads:
            finish(head - lag, *weights.pop(head - lag))


def project_kernel(rows_ref, wk_ref, wv_ref, k_ref, v_ref):
    rows = rows_ref[...].reshape(-1, rows_ref.shape[-1])
    for w_ref, target in ((wk_ref, k_ref), (wv_ref, v_ref)):
        target[...] = jnp.dot(rows, w_ref[...], preferred_element_type=F32).astype(BF16).reshape(target.shape)


def project(rows, wk, wv):
    count, feat = rows.shape[0] // NEIGHBOURS, wk.shape[1]
    shape = jax.ShapeDtypeStruct((count, NEIGHBOURS * rows.shape[1], feat), BF16)
    return pl.pallas_call(
        project_kernel,
        in_specs=[VMEM] * 3,
        out_specs=[VMEM] * 2,
        out_shape=[shape] * 2,
        compiler_params=params(16),
        name="project_rows",
    )(rows, wk, wv)


def attend_kernel(start, count, sources, pair, done, id_ref, *refs):
    refs = list(refs)
    take = lambda n: [refs.pop(0) for _ in range(n)]
    row_refs = take(sources)
    ready = take(2 if done else 0)
    wk_ref, wv_ref, q_ref, go_ref = take(4)
    out_ref, gq_ref, turned = take(3)
    grad_refs = take(2 * PIECES)
    keys, values, rows, ranks = take(4)
    size, width = rows.shape[1:]
    part, feat = keys.shape[1:]
    if pair:
        for i, ref in enumerate(row_refs):
            rows[:, i * (size // 2) : (i + 1) * (size // 2)] = ref[...].reshape(count, size // 2, width)
    else:
        place_rows(start, count, id_ref, row_refs, ranks, lambda i: rows.at[i // NEIGHBOURS, pl.ds(i % NEIGHBOURS * NEIGH_LEN, NEIGH_LEN)])

    rest = (row_refs[1] if done else rows)[...].reshape(-1, width)
    for w_ref, target in ((wk_ref, keys), (wv_ref, values)):
        product = jnp.dot(rest, w_ref[...], preferred_element_type=F32).astype(BF16)
        target[...] = product.reshape(count, part, feat)

    def block(b, carry):
        def pick(at, *parts):
            return lambda cols: jnp.concatenate([ref[at, :, cols] for ref in parts], axis=0)

        context = pick(b, *ready[:1], keys), pick(b, *ready[1:], values)
        block_grads(*context, pick(start + b, q_ref), pick(start + b, go_ref), out_ref.at[b], gq_ref.at[b], [ref.at[b] for ref in grad_refs])
        return carry

    lax.fori_loop(0, count, block, 0)
    turned[...] = rows[...].reshape(-1, width).T


def attend(rows, ready, own, wk, wv, queries, grad_out, start, count, pair):
    _, tokens, feat = queries.shape
    enc = wk.shape[0]
    context = NEIGHBOURS * NEIGH_LEN
    row_shape = jax.ShapeDtypeStruct((count, tokens, feat), BF16)
    if not pair:
        rows = [part.reshape(part.shape[0], NEIGH_LEN, enc) for part in rows]
    turned_shape = jax.ShapeDtypeStruct((enc, count * context), BF16)
    bounds = piece_heads(feat // HEAD_DIM)
    widths = [(bounds[piece + 1] - bounds[piece]) * HEAD_DIM for piece in range(PIECES) for _ in range(2)]
    grad_shapes = [jax.ShapeDtypeStruct((count, context, width), BF16) for width in widths]
    fresh = context // 2 if ready else context
    settings = start, count, len(rows), pair, bool(ready)
    return pl.pallas_call(
        functools.partial(attend_kernel, *settings),
        in_specs=[SMEM] + [VMEM] * (len(rows) + len(ready) + 4),
        out_specs=[VMEM] * (3 + 2 * PIECES),
        scratch_shapes=[
            pltpu.VMEM((count, fresh, feat), BF16),
            pltpu.VMEM((count, fresh, feat), BF16),
            pltpu.VMEM((count, context, enc), BF16),
            pltpu.SMEM((len(rows),), jnp.int32),
        ],
        out_shape=[row_shape, row_shape, turned_shape] + grad_shapes,
        compiler_params=params(ATTEND_MIB),
        name="attend_blocks",
    )(own, *rows, *ready, wk, wv, queries, grad_out)


def weigh_kernel(chunks, streams, carried, sides, *refs):
    refs = list(refs)
    take = lambda n: [refs.pop(0) for _ in range(n)]
    turned, grads = take(chunks), [take(chunks) for _ in range(streams)]
    before = take(streams) if carried else []
    enc = turned[0].shape[0]
    for side in sides:
        rows = slice(0, enc)
        if side is not None:
            half = lax.axis_index("dp") if side else 1 - lax.axis_index("dp")
            rows = pl.ds(pl.multiple_of(half * (enc // 2), enc // 2), enc // 2)
        for i in range(streams):
            total = before[i][rows, :] if carried else 0.0
            for turn, ref in zip(turned, grads[i]):
                grad = ref[...]
                total += jnp.dot(turn[rows, :], grad.reshape(-1, grad.shape[-1]), preferred_element_type=F32)
            target = refs.pop(0)
            target[...] = total.astype(target.dtype)


def weigh(turned, grads, before, sides):
    enc, width = turned[0].shape[0], grads[0][0].shape[-1]
    shapes = [
        jax.ShapeDtypeStruct((enc, width), F32) if side is None else jax.ShapeDtypeStruct((enc // 2, width), BF16)
        for side in sides
        for _ in grads
    ]
    return pl.pallas_call(
        functools.partial(weigh_kernel, len(turned), len(grads), bool(before), sides),
        in_specs=[VMEM] * ((1 + len(grads)) * len(turned) + len(before)),
        out_specs=[VMEM] * len(shapes),
        out_shape=shapes,
        compiler_params=params(WEIGH_MIB),
        name="weigh_grads",
    )(*turned, *sum(grads, []), *before)


def fold_kernel(dims, count, *refs):
    ret = lax.axis_index("ret")
    for i in range(count):
        held_ref, arrived_ref = refs[i], refs[count + i]
        bit, place = dims[i]
        mine = (ret >> bit) & 1
        stride = 1 << place
        for j in range(held_ref.shape[0] // 2):
            base = (j // stride) * 2 * stride + j % stride
            for k, side in enumerate((1 - mine, mine)):
                row = base + side * stride
                total = held_ref[row].astype(F32) + arrived_ref[row].astype(F32)
                refs[(2 + k) * count + i][j] = total.astype(BF16)


def fold(held, arrived, dims):
    count = len(held)
    parts, rows, width = held[0].shape
    shapes = [jax.ShapeDtypeStruct((parts // 2, rows, width), BF16)] * (2 * count)
    return pl.pallas_call(
        functools.partial(fold_kernel, dims, count),
        in_specs=[VMEM] * (2 * count),
        out_specs=[VMEM] * len(shapes),
        out_shape=shapes,
        compiler_params=params(16),
        name="fold_grads",
    )(*held, *arrived)


def join_kernel(*refs):
    count = (len(refs) - 2) // 2
    place = [0, 0]
    for i in range(count):
        total = refs[i][0].astype(F32) + refs[count + i][0].astype(F32)
        width = total.shape[1]
        refs[2 * count + i % 2][:, place[i % 2] : place[i % 2] + width] = total
        place[i % 2] += width


def join(held, arrived):
    rows, feat = held[0].shape[1], sum(part.shape[2] for part in held) // 2
    return pl.pallas_call(
        join_kernel,
        in_specs=[VMEM] * (2 * len(held)),
        out_specs=[VMEM] * 2,
        out_shape=[jax.ShapeDtypeStruct((rows, feat), F32)] * 2,
        compiler_params=params(16),
        name="join_grads",
    )(*held, *arrived)


class Sums:
    def __init__(self, send, held):
        self.bits = lax.axis_size("ret").bit_length() - 1
        self.left = [list(range(self.bits)) for _ in held]
        self.held = self.split(held)
        self.arrived = self.split([swap(grad, "dp", 1) for grad in send])
        self.steps = 0

    def split(self, grads):
        return [grad.reshape(1 << self.bits, -1, grad.shape[-1]) for grad in grads]

    def fold(self):
        self.bit = [self.steps, self.bits - 1 - self.steps]
        dims = tuple((bit, left.index(bit)) for bit, left in zip(self.bit, self.left))
        for bit, left in zip(self.bit, self.left):
            left.remove(bit)
        parts = [fold([held], [arrived], (dim,)) for held, arrived, dim in zip(self.held, self.arrived, dims)]
        self.send, self.held = ([part[i] for part in parts] for i in range(2))
        self.steps += 1

    def exchange(self):
        self.arrived = [swap(grad, "ret", 1 << bit) for grad, bit in zip(self.send, self.bit)]


def spans_of(blocks):
    spans, start = [], 0
    for count, pair in CHUNKS:
        spans.append((start, count, pair))
        start += count
    return spans if start == blocks else [(0, blocks, False)]


def local(queries, enc_states, w_key, w_value, shard_ids, row_ids, grad_out):
    n_ret = lax.axis_size("ret")
    blocks = shard_ids.shape[1]
    bound = blocks * NEIGHBOURS * 2 // n_ret
    enc = enc_states.shape[2]

    def capacity(count):
        return min(count, bound)

    own = jnp.stack([shard_ids[0], row_ids[0]], axis=-1).reshape(-1)
    ids = exchange_ids(own)
    normed = normalize_rows(enc_states[0]).reshape(-1, 2, HALF, enc)
    spans = spans_of(blocks)
    outgoing = pick(ids, normed, spans[:1], capacity)
    if len(spans) > 1:
        outgoing = outgoing + pick(ids, normed, spans[1:], capacity)
    query_blocks, grad_blocks = (array.reshape(blocks, -1, array.shape[2]) for array in (queries, grad_out))
    attended, grad_queries, arrivals = [], [], []
    for slots in outgoing:
        slots = list(slots)
        if arrivals:
            for k in range(1, n_ret):
                arrivals[-1][k], slots[k] = lax.optimization_barrier((arrivals[-1][k], slots[k]))
        arrivals.append(slots[:1] + [swap(slots[k], "ret", k) for k in range(1, n_ret)])
    rows, turned, found, sums, early = [None] * len(spans), [], [], [[]] * PIECES, None
    ready = [[] for _ in spans]

    def weigh_piece(turned, found, piece, before, sides, streams=(0, 1)):
        before = [before[i] for i in streams] if before else []
        return list(weigh(turned, [[grads[2 * piece + i] for grads in found] for i in streams], before, sides))


    def prepare(i):
        start, count, pair = spans[i]
        if pair:
            mine = unpack(own, arrivals[i], start, count)
            rows[i] = [mine, swap(mine, "ctx", 1)]
            if PROJECT_FIRST:
                ready[i] = list(project(mine, w_key, w_value))
        else:
            rows[i] = arrivals[i]

    prepare(0)
    for i, (start, count, pair) in enumerate(spans):
        last = i + 1 == len(spans)
        if not last and spans[i + 1][2]:
            if ready[i]:
                ready[i][0], arrivals[i + 1] = lax.optimization_barrier((ready[i][0], arrivals[i + 1]))
            prepare(i + 1)
            rows[i][0], rows[i + 1][0] = lax.optimization_barrier((rows[i][0], rows[i + 1][0]))
        results = attend(rows[i], ready[i], own, w_key, w_value, query_blocks, grad_blocks, start, count, pair)
        out, gq, flipped, *grads = results
        attended.append(out)
        grad_queries.append(gq)
        turned.append(flipped)
        found.append(grads)
        if i == 0 and not last:
            early = turned, found
            turned, found = [], []
            sums[0] = weigh_piece(*early, 0, [], (None,))
            sums[0][0], rows[1][0] = lax.optimization_barrier((sums[0][0], rows[1][0]))
        if not last and rows[i + 1] is None:
            attended[-1], arrivals[i + 1] = lax.optimization_barrier((attended[-1], arrivals[i + 1]))
            prepare(i + 1)
    states = []
    for piece in range(PIECES):
        if piece:
            if early:
                parts[0], early[0][0] = lax.optimization_barrier((parts[0], early[0][0]))
                sums[piece] = weigh_piece(*early, piece, [], (None,))
            states.append(Sums(parts[:2], parts[2:]))
            states[-1].fold()
            states[-1].send, turned[0] = lax.optimization_barrier((states[-1].send, turned[0]))
        parts = []
        for sides, streams in SIDES[piece]:
            parts += weigh_piece(turned, found, piece, sums[piece], sides, streams)
    states.append(Sums(parts[:2], parts[2:]))
    states[-1].fold()
    for step in range(states[0].bits):
        for state in states:
            if step:
                state.fold()
            state.exchange()
    grad_w_key, grad_w_value = join(sum([state.held for state in states], []), sum([state.arrived for state in states], []))
    attended, grad_queries = (jnp.concatenate(blocks).reshape(queries.shape) for blocks in (attended, grad_queries))
    return attended, grad_queries, grad_w_key, grad_w_value


def solution(mesh):
    placed = (
        P("dp", "ret", "ctx"),
        P("dp", "ret", None),
        P(None, "ctx"),
        P(None, "ctx"),
        P("dp", "ret", None),
        P("dp", "ret", None),
        P("dp", "ret", "ctx"),
    )
    return jax.shard_map(
        local,
        mesh=mesh,
        in_specs=placed,
        out_specs=(
            P("dp", "ret", "ctx"),
            P("dp", "ret", "ctx"),
            P(("dp", "ret"), "ctx"),
            P(("dp", "ret"), "ctx"),
        ),
        check_vma=False,
    )
```
